256 devices in a mesh: lon: 32 (over z, x_lo, core), lat: 8 (over y, x_hi).
Axes of the slice: x: 4 (x_hi: 2, x_lo: 2; x = x_hi * 2 + x_lo), y: 4, z: 8, core: 2. Of those that a mesh axis runs over, the one named last changes fastest.
Arguments:
- tokens: bfloat16 [3, 192, 384, 512], P(None, 'lat', 'lon'), may hold values from -6 to 6
- valid: int32 [192, 384], replicated, may hold values 0 or 1
- w_qkv1: bfloat16 [512, 1536], P('lon'), may hold values from -0.25 to 0.25
- w_out1: bfloat16 [512, 512], P('lon'), may hold values from -0.25 to 0.25
- w_merge: bfloat16 [2048, 1024], P('lon'), may hold values from -0.125 to 0.125
- w_qkv2: bfloat16 [1024, 3072], P('lon'), may hold values from -0.1875 to 0.1875
- w_out2: bfloat16 [1024, 1024], P('lon'), may hold values from -0.1875 to 0.1875
- w_up: bfloat16 [1024, 2048], P('lon'), may hold values from -0.1875 to 0.1875
- gain1: float32 [512], replicated, may hold values from 0.5 to 2
- gain_merge: float32 [2048], replicated, may hold values from 0.5 to 2
- gain2: float32 [1024], replicated, may hold values from 0.5 to 2
- gain_up: float32 [512], replicated, may hold values from 0.5 to 2
- out_cot: bfloat16 [3, 192, 384, 512], P(None, 'lat', 'lon'), may hold values from -6 to 6
Outputs:
- output: bfloat16 [3, 192, 384, 512], P(None, 'lat', 'lon')
- grad_tokens: bfloat16 [3, 192, 384, 512], P(None, 'lat', 'lon')
The draws below stay inside these ranges and needn't reach their ends.
All inputs are finite; a program needn't handle non-finite values.
Results may differ from the reference program's by a relative error of at most 0.039.
Values may be sent and summed in bfloat16 or wider, within the bound.
A program may use at most 192 MiB of HBM per device.

```python
import math
import jax
import jax.numpy as jnp
from jax import lax

D1 = 512
D2 = 1024
HD = 32
LEV = 3
WLAT = 6
WLON = 6
NLAT = 192
NLON = 384


def touch_ends(values, own_key, least, high):
    longest = values.shape.index(max(values.shape))
    spots = []
    for shift in (0, 1):
        where = [jax.random.randint(jax.random.fold_in(own_key, axis), (), 0, length) for axis, length in enumerate(values.shape)]
        where[longest] = (where[longest] + shift) % values.shape[longest]
        spots.append(tuple(where))
    return values.at[spots[0]].set(least).at[spots[1]].set(high)


def level_of(rng, shape, pieces, low, top_value):
    def one(position, shards_of):
        steps = jax.random.uniform(jax.random.fold_in(jax.random.fold_in(rng, 6), position), (shards_of,), jnp.float32, low / len(pieces), top_value / len(pieces))
        return jnp.repeat(jnp.exp(steps), shape[position] // shards_of).reshape((-1,) + (1,) * (len(shape) - position - 1))

    level = one(*pieces[0])
    for cut in pieces[1:]:
        level = level * one(*cut)
    return level


def bell_draw(key, extent, scale, bound, cuts=(), kind=jnp.bfloat16):
    array = scale * jax.random.normal(key, extent, jnp.float32)
    if cuts:
        array = array * level_of(key, extent, cuts, -0.22, 0.18)
    return jnp.clip(array, -bound, bound).astype(kind)


def setup_inputs(seed: int = 0) -> dict:
    key_of = jax.random.split(jax.random.key(seed), 14)
    tokens = bell_draw(key_of[0], (LEV, NLAT, NLON, D1), 1.0, 6.0, ((1, 8), (2, 32)))
    valid = touch_ends((jax.random.randint(key_of[1], (NLAT, NLON), 0, 4) < 3).astype(jnp.int32), jax.random.fold_in(key_of[1], 1), 0, 1)
    w_qkv1 = bell_draw(key_of[2], (D1, 3 * D1), D1 ** -0.5, 0.25, ((0, 32),))
    w_out1 = bell_draw(key_of[3], (D1, D1), D1 ** -0.5, 0.25, ((0, 32),))
    w_merge = bell_draw(key_of[4], (4 * D1, D2), (4 * D1) ** -0.5, 0.125, ((0, 32),))
    w_qkv2 = bell_draw(key_of[5], (D2, 3 * D2), D2 ** -0.5, 0.1875, ((0, 32),))
    w_out2 = bell_draw(key_of[6], (D2, D2), D2 ** -0.5, 0.1875, ((0, 32),))
    w_up = bell_draw(key_of[7], (D2, 4 * D1), D2 ** -0.5, 0.1875, ((0, 32),))
    gain1 = jnp.clip(jnp.exp(jax.random.uniform(key_of[8], (D1,), jnp.float32, math.log(0.5), math.log(2.0))), 0.5, 2.0)
    gain_merge = jnp.clip(jnp.exp(jax.random.uniform(key_of[9], (4 * D1,), jnp.float32, math.log(0.5), math.log(2.0))), 0.5, 2.0)
    gain2 = jnp.clip(jnp.exp(jax.random.uniform(key_of[10], (D2,), jnp.float32, math.log(0.5), math.log(2.0))), 0.5, 2.0)
    gain_up = jnp.clip(jnp.exp(jax.random.uniform(key_of[11], (D1,), jnp.float32, math.log(0.5), math.log(2.0))), 0.5, 2.0)
    out_cot = bell_draw(key_of[12], (LEV, NLAT, NLON, D1), 1.0, 6.0, ((1, 8), (2, 32)))
    return dict(tokens=tokens, valid=valid, w_qkv1=w_qkv1, w_out1=w_out1, w_merge=w_merge, w_qkv2=w_qkv2, w_out2=w_out2, w_up=w_up, gain1=gain1, gain_merge=gain_merge, gain2=gain2, gain_up=gain_up, out_cot=out_cot)


EPS = 1e-05

def norm_rows(values, gain):
    values = values.astype(jnp.float32)
    center = values - lax.optimization_barrier(jnp.mean(values, axis=-1, keepdims=True))
    spread = lax.optimization_barrier(jnp.mean(center * center, axis=-1, keepdims=True))
    return center * lax.rsqrt(spread + EPS) * gain

def to_windows(field):
    levels, rows, columns, width = field.shape
    field = field.reshape(levels, rows // WLAT, WLAT, columns // WLON, WLON, width)
    field = field.transpose(1, 3, 0, 2, 4, 5)
    return field.reshape(rows // WLAT, columns // WLON, levels * WLAT * WLON, width)

def from_windows(blocks, levels):
    band_count, block_count, tokens_in, width = blocks.shape
    blocks = blocks.reshape(band_count, block_count, levels, WLAT, WLON, width)
    blocks = blocks.transpose(2, 0, 3, 1, 4, 5)
    return blocks.reshape(levels, band_count * WLAT, block_count * WLON, width)

def grid_windows(grid, levels):
    widened = jnp.broadcast_to(grid[None, :, :, None], (levels,) + grid.shape + (1,))
    return to_windows(widened)[..., 0]

def mask_grids(usable, shift_rows, shift_columns):
    rows = usable.shape[0]
    rolled = jnp.roll(usable, (-shift_rows, -shift_columns), (0, 1))
    place = jnp.arange(rows, dtype=jnp.int32)
    region = (place >= rows - WLAT).astype(jnp.int32) + (place >= rows - shift_rows).astype(jnp.int32)
    return (jnp.broadcast_to(region[:, None], rolled.shape), rolled)

def coarse_usable(usable):
    rows, columns = usable.shape
    return lax.optimization_barrier(jnp.max(usable.reshape(rows // 2, 2, columns // 2, 2), axis=(1, 3)))

def roll_grid(field, sign):
    return jnp.roll(field, (sign * (WLAT // 2), sign * (WLON // 2)), (1, 2))

def attend(field, w_qkv, w_out, region, usable, heads):
    count, tokens_in, width = field.shape
    head_size = width // heads
    mixed = jnp.dot(field.reshape(count * tokens_in, width), w_qkv, preferred_element_type=jnp.float32)
    mixed = mixed.astype(jnp.bfloat16).reshape(count, tokens_in, 3, heads, head_size)
    query, keys, values = (mixed[:, :, 0], mixed[:, :, 1], mixed[:, :, 2])
    scores = jnp.einsum('bihe,bjhe->bhij', query.astype(jnp.float32), keys.astype(jnp.float32)) * head_size ** (-0.5)
    same = region[:, :, None] == region[:, None, :]
    allowed = same & ((usable[:, None, :] > 0) | jnp.eye(tokens_in, dtype=bool)[None])
    raised = jnp.where(allowed[:, None], jnp.exp(scores), 0.0)
    probs = (raised / lax.optimization_barrier(jnp.sum(raised, axis=-1, keepdims=True))).astype(jnp.bfloat16)
    heads_out = jnp.einsum('bhij,bjhe->bihe', probs.astype(jnp.float32), values.astype(jnp.float32))
    heads_out = heads_out.astype(jnp.bfloat16).reshape(count * tokens_in, width)
    result = jnp.dot(heads_out, w_out, preferred_element_type=jnp.float32)
    return result.astype(jnp.bfloat16).reshape(count, tokens_in, width)

def section_attention(field, w_qkv, w_out, region, usable, heads):
    levels = field.shape[0]
    blocks = to_windows(field)
    region_blocks = grid_windows(region, levels)
    usable_blocks = grid_windows(usable, levels)

    def one_band(items):
        return attend(items[0], w_qkv, w_out, items[1], items[2], heads)
    return from_windows(lax.map(one_band, (blocks, region_blocks, usable_blocks)), levels)

def section_attention_back(field, cotangent, w_qkv, w_out, region, usable, heads):
    levels = field.shape[0]
    blocks = to_windows(field)
    cot_blocks = to_windows(cotangent)
    region_blocks = grid_windows(region, levels)
    usable_blocks = grid_windows(usable, levels)

    def one_band(items):

        def local(part):
            return attend(part, w_qkv, w_out, items[2], items[3], heads)
        unused, pull = jax.vjp(local, items[0])
        return pull(items[1])[0]
    return from_windows(lax.map(one_band, (blocks, cot_blocks, region_blocks, usable_blocks)), levels)

def merge_piece(field, added, w_merge, gain_merge, gain2):
    stream = (field.astype(jnp.float32) + added.astype(jnp.float32)).astype(jnp.bfloat16)
    levels, rows, columns, width = stream.shape
    patches = stream.reshape(levels, rows // 2, 2, columns // 2, 2, width).transpose(0, 1, 3, 2, 4, 5)
    patches = patches.reshape(levels, rows // 2, columns // 2, 4 * width)
    merged = norm_rows(patches, gain_merge).astype(jnp.bfloat16)
    coarse = jnp.dot(merged.reshape(-1, 4 * width), w_merge, preferred_element_type=jnp.float32)
    coarse = coarse.astype(jnp.bfloat16).reshape(levels, rows // 2, columns // 2, w_merge.shape[1])
    normed = norm_rows(coarse, gain2).astype(jnp.bfloat16)
    return (stream, coarse, normed)

def up_piece(coarse, added, skip, w_up, gain_up):
    upper = (coarse.astype(jnp.float32) + added.astype(jnp.float32)).astype(jnp.bfloat16)
    levels, rows, columns, width = upper.shape
    fine_width = w_up.shape[1] // 4
    spread = jnp.dot(upper.reshape(-1, width), w_up, preferred_element_type=jnp.float32)
    spread = spread.reshape(levels, rows, columns, 2, 2, fine_width).transpose(0, 1, 3, 2, 4, 5)
    spread = spread.reshape(levels, 2 * rows, 2 * columns, fine_width)
    return (skip.astype(jnp.float32) + norm_rows(spread, gain_up)).astype(jnp.bfloat16)

def reference(tokens, valid, w_qkv1, w_out1, w_merge, w_qkv2, w_out2, w_up, gain1, gain_merge, gain2, gain_up, out_cot):
    heads_first = D1 // HD
    heads_second = D2 // HD
    region1, usable1 = mask_grids(valid, WLAT // 2, WLON // 2)
    region2, usable2 = mask_grids(coarse_usable(valid), WLAT // 2, WLON // 2)

    def first(field):
        return norm_rows(field, gain1).astype(jnp.bfloat16)
    normed1, pull_first = jax.vjp(first, tokens)
    rolled1 = roll_grid(normed1, -1)
    back1 = roll_grid(section_attention(rolled1, w_qkv1, w_out1, region1, usable1, heads_first), 1)

    def middle(field, added):
        return merge_piece(field, added, w_merge, gain_merge, gain2)
    (stream, coarse, normed2), pull_middle = jax.vjp(middle, tokens, back1)
    rolled2 = roll_grid(normed2, -1)
    back2 = roll_grid(section_attention(rolled2, w_qkv2, w_out2, region2, usable2, heads_second), 1)

    def last(base, added, skip):
        return up_piece(base, added, skip, w_up, gain_up)
    output, pull_last = jax.vjp(last, coarse, back2, stream)
    grad_coarse, grad_back2, grad_stream = pull_last(out_cot)
    grad_rolled2 = section_attention_back(rolled2, roll_grid(grad_back2, -1), w_qkv2, w_out2, region2, usable2, heads_second)
    grad_normed2 = roll_grid(grad_rolled2, 1)
    grad_middle, grad_back1 = pull_middle((grad_stream, grad_coarse, grad_normed2))
    grad_rolled1 = section_attention_back(rolled1, roll_grid(grad_back1, -1), w_qkv1, w_out1, region1, usable1, heads_first)
    grad_first = pull_first(roll_grid(grad_rolled1, 1))[0]
    grad_tokens = (grad_middle.astype(jnp.float32) + grad_first.astype(jnp.float32)).astype(jnp.bfloat16)
    return (output, grad_tokens)
```

```python
import functools

import jax
import jax.numpy as jnp
import numpy as np
from jax import lax
from jax.experimental import pallas as pl
from jax.experimental.pallas import tpu as pltpu
from jax.sharding import PartitionSpec as P

EPS = 1e-05
BF = jnp.bfloat16
F32 = jnp.float32
LONS = 32
MIB = 1024 * 1024

PACK = {
    "qkv2": (0, 32, 24),
    "out2": (768, 32, 8),
    "merge": (1024, 64, 8),
    "up": (1536, 32, 16),
    "out1": (2048, 16, 4),
    "qkv1": (2112, 16, 12),
}
PACK_ROWS = 2304
SCALE = 32.0**-0.5
LOG2E = 1.4426950408889634
BLOCKED = -1e30


def permutations():
    merge_of_raw = np.zeros((256, 288), np.float32)
    quarter_of_merge = np.zeros((128, 128), np.float32)
    for level in range(3):
        for row in range(6):
            for column in range(6):
                member = (row % 2) * 2 + column % 2
                merge_at = member * 32 + level * 9 + (row // 2) * 3 + column // 2
                quarter = (row // 3) * 2 + column // 3
                quarter_at = quarter * 32 + level * 9 + (row % 3) * 3 + column % 3
                quarter_of_merge[quarter_at, merge_at] = 1
                for half in range(2):
                    raw_at = level * 96 + row * 16 + half * 6 + column
                    merge_of_raw[half * 128 + merge_at, raw_at] = 1
    return merge_of_raw, quarter_of_merge


def nn(a, b):
    return lax.dot_general(a, b, (((1,), (0,)), ((), ())), preferred_element_type=F32)


def nt(a, b):
    return lax.dot_general(a, b, (((1,), (1,)), ((), ())), preferred_element_type=F32)


def tn(a, b):
    return lax.dot_general(a, b, (((0,), (0,)), ((), ())), preferred_element_type=F32)


def weight_columns(ref, rows, tile, count):
    parts = []
    for step in range(count):
        start = pl.multiple_of((tile + step) * rows, rows)
        parts.append(ref[:, pl.ds(start, rows), :].reshape(LONS * rows, 128))
    return jnp.concatenate(parts, axis=1) if count > 1 else parts[0]


def weight_rows(ref, rows, tiles, first, count):
    shards = pl.ds(first // rows, count // rows)
    parts = [ref[shards, tile * rows : (tile + 1) * rows, :].reshape(count, 128) for tile in range(tiles)]
    return jnp.concatenate(parts, axis=1)


def norm_parts(values):
    center = values - jnp.mean(values, axis=-1, keepdims=True)
    scale = lax.rsqrt(jnp.mean(center * center, axis=-1, keepdims=True) + EPS)
    return center * scale, scale


def norm_back(hat, scale, pulled):
    down = jnp.mean(pulled, axis=-1, keepdims=True)
    along = jnp.mean(pulled * hat, axis=-1, keepdims=True)
    return scale * (pulled - down - hat * along)


def pack_kernel(qkv1, out1, merge, qkv2, out2, up, packed):
    for name, ref in (("qkv1", qkv1), ("out1", out1), ("merge", merge), ("qkv2", qkv2), ("out2", out2), ("up", up)):
        first, rows, tiles = PACK[name]
        for tile in range(tiles):
            packed[first + tile * rows : first + (tile + 1) * rows, :] = ref[:, tile * 128 : (tile + 1) * 128]


def ahead(own, lon, lat, diag, row, column):
    rows, columns = own.shape[0], own.shape[1]
    if row < rows and column < columns:
        return own.at[row, column]
    if row < rows:
        return lon.at[row]
    if column < columns:
        return lat.at[column]
    return diag.at[0]


def behind(own, lon, lat, diag, row, column):
    if row and column:
        return own.at[row, column]
    if row:
        return lon.at[row]
    if column:
        return lat.at[column]
    return diag.at[0]


def put_quarters(own, lon, lat, diag, row, column, value):
    own[row, column] = value
    if column == 0:
        lon[row] = value
    if row == 0:
        lat[column] = value
    if row == 0 and column == 0:
        diag[0] = value


def window_spots(rows, columns):
    for row in range(1, rows + 1):
        for column in range(1, columns + 1):
            window = (row - 1) // 2 * (columns // 2) + (column - 1) // 2
            yield row, column, window, ((row - 1) % 2 * 2 + (column - 1) % 2) * 32


def enter_kernel(tokens, cot, gain, merge_of_raw, quarter_of_merge, tokens_m, cot_m, own, lon, lat, diag, padded):
    padded[...] = jnp.zeros_like(padded)
    bands = tokens.shape[1] // 6
    padded[:, :, 0:12, :] = cot[...]
    for band in range(bands):
        rows = padded[:, band * 6 : band * 6 + 6].reshape(288, 512)
        cot_m[2 * band : 2 * band + 2] = nn(merge_of_raw[...], rows).astype(BF).reshape(2, 128, 512)
    padded[:, :, 0:12, :] = tokens[...]
    for band in range(bands):
        rows = padded[:, band * 6 : band * 6 + 6].reshape(288, 512)
        moved = nn(merge_of_raw[...], rows)
        tokens_m[2 * band : 2 * band + 2] = moved.astype(BF).reshape(2, 128, 512)
        hat, _ = norm_parts(moved)
        normed = (hat * gain[...]).astype(BF)
        for half in range(2):
            quarters = nn(quarter_of_merge[...], normed[half * 128 : half * 128 + 128]).astype(BF)
            for quarter in range(4):
                row, column = 2 * band + quarter // 2, 2 * half + quarter % 2
                put_quarters(own, lon, lat, diag, row, column, quarters[quarter * 32 : quarter * 32 + 32])


def head_masks():
    lane = lax.broadcasted_iota(jnp.int32, (1, 128), 1) // 32
    return [lane == head for head in range(4)]


def window_bias(usable_ref, flag_ref, window, windows, per_band):
    me = lax.broadcasted_iota(jnp.int32, (128, 128), 0)
    key = lax.broadcasted_iota(jnp.int32, (128, 128), 1)
    usable = usable_ref[pl.ds(window, 1), 0, :]
    cut = (flag_ref[0, 0] * jnp.where(window >= windows - per_band, 1, 0)).astype(jnp.int32)
    apart = jnp.where((me // 64) == (key // 64), 0, 1) * cut
    allowed = ((usable > 0.0) | (me == key)) & (apart == 0)
    return jnp.where(allowed, 0.0, BLOCKED)


def attend_kernel(
    own, lon, lat, diag, w_qkv, w_out, usable, flag,
    own_o, lon_o, lat_o, diag_o, qkv, raised, inverse, heads_out, field,
):
    rows, columns, _, width = own.shape
    windows = rows * columns // 4
    tiles = width // 128
    shard = width // LONS
    for row, column, window, at in window_spots(rows, columns):
        field[window, at : at + 32, :] = ahead(own, lon, lat, diag, row, column)[...]

    def project(step, carry):
        weight = weight_columns(w_qkv, shard, 2 * step, 2)
        mixed = nn(field[...].reshape(windows * 128, width), weight).astype(BF)
        qkv[2 * step] = mixed[:, :128].reshape(windows, 128, 128)
        qkv[2 * step + 1] = mixed[:, 128:].reshape(windows, 128, 128)
        return carry

    lax.fori_loop(0, 3 * tiles // 2, project, 0)
    masks = head_masks()
    zero = jnp.zeros((), BF)
    ones = jnp.ones((128, 128), BF)

    def window_step(window, carry):
        bias = window_bias(usable, flag, window, windows, columns // 2)
        bias = jnp.concatenate([bias] * 4, axis=0)

        def tile_step(tile, carry):
            query, keys, values = qkv[tile, window], qkv[tiles + tile, window], qkv[2 * tiles + tile, window]
            queries = jnp.concatenate([jnp.where(mask, query, zero) for mask in masks], axis=0)
            power = jnp.exp2(nt(queries, keys) * (SCALE * LOG2E) + bias).astype(BF)
            raised[window, tile] = power
            side = jnp.concatenate([power[128 * head : 128 * head + 128] for head in range(4)], axis=1)
            stacked = jnp.concatenate(
                [
                    jnp.concatenate([jnp.where(mask, values, zero), jnp.where(mask, ones, zero)], axis=1)
                    for mask in masks
                ],
                axis=0,
            )
            both = nn(side, stacked)
            share = 1.0 / both[:, 128:]
            inverse[window, tile] = share
            heads_out[tile, window] = (both[:, :128] * share).astype(BF)
            return carry

        return lax.fori_loop(0, tiles, tile_step, carry)

    lax.fori_loop(0, windows, window_step, 0)
    heads = jnp.concatenate([heads_out[tile].reshape(windows * 128, 128) for tile in range(tiles)], axis=1)
    for step in range(tiles // 2):
        result = nn(heads, weight_columns(w_out, shard, 2 * step, 2)).astype(BF)
        for row, column, window, at in window_spots(rows, columns):
            target = ahead(own_o, lon_o, lat_o, diag_o, row, column)
            target[:, step * 256 : step * 256 + 256] = result[window * 128 + at : window * 128 + at + 32]


def attend_back_kernel(
    own, lon, lat, diag, w_qkv, w_out, qkv, raised, inverse, heads_out,
    own_o, lon_o, lat_o, diag_o, field, pulled,
):
    rows, columns, _, width = own.shape
    windows = rows * columns // 4
    tiles = width // 128
    shard = width // LONS
    for row, column, window, at in window_spots(rows, columns):
        field[window, at : at + 32, :] = ahead(own, lon, lat, diag, row, column)[...]
    for step in range(tiles // 2):
        part = nt(field[...].reshape(windows * 128, width), weight_rows(w_out, shard, tiles, 256 * step, 256))
        part = part.astype(BF)
        pulled[2 * step] = part[:, :128].reshape(windows, 128, 128)
        pulled[2 * step + 1] = part[:, 128:].reshape(windows, 128, 128)
    masks = head_masks()
    zero = jnp.zeros((), BF)
    ones = jnp.ones((128, 128), BF)

    def stack(values):
        return jnp.concatenate([jnp.where(mask, values, zero) for mask in masks], axis=0)

    def tile_step(index, carry):
        window, tile = index // tiles, index % tiles
        query, keys, values = qkv[tile, window], qkv[tiles + tile, window], qkv[2 * tiles + tile, window]
        power = raised[window, tile]
        scaled = pulled[tile, window].astype(F32) * inverse[window, tile]
        taken = (scaled * heads_out[tile, window].astype(F32)).astype(BF)
        scaled_rows = stack(scaled.astype(BF))
        left = jnp.concatenate([scaled_rows, stack(-taken)], axis=1)
        slope = nt(left, jnp.concatenate([values, ones], axis=1))
        slope = (power.astype(F32) * slope).astype(BF)
        side = jnp.concatenate([slope[128 * head : 128 * head + 128] for head in range(4)], axis=1)
        pulled[2 * tiles + tile, window] = tn(power, scaled_rows).astype(BF)
        pulled[tiles + tile, window] = (tn(slope, stack(query)) * SCALE).astype(BF)
        pulled[tile, window] = (nn(side, stack(keys)) * SCALE).astype(BF)
        return carry

    lax.fori_loop(0, windows * tiles, tile_step, 0)
    pulls = jnp.concatenate([pulled[tile].reshape(windows * 128, 128) for tile in range(3 * tiles)], axis=1)
    for step in range(tiles // 2):
        result = nt(pulls, weight_rows(w_qkv, shard, 3 * tiles, 256 * step, 256)).astype(BF)
        for row, column, window, at in window_spots(rows, columns):
            target = ahead(own_o, lon_o, lat_o, diag_o, row, column)
            target[:, step * 256 : step * 256 + 256] = result[window * 128 + at : window * 128 + at + 32]


def coarse_quarters():
    for cell in range(8):
        yield cell, cell // 2, cell % 2


def fine_block(own, lon, lat, diag, row, column):
    parts = [behind(own, lon, lat, diag, 2 * row + q // 2, 2 * column + q % 2)[...] for q in range(4)]
    return jnp.concatenate(parts, axis=0)


def members(block):
    return jnp.concatenate([block[32 * m : 32 * m + 32] for m in range(4)], axis=1)


def merge_kernel(
    own, lon, lat, diag, tokens_m, w_merge, gain_merge, gain2, merge_of_quarter,
    stream, coarse, own_o, lon_o, lat_o, diag_o, merged, total,
):
    for cell, row, column in coarse_quarters():
        added = nn(merge_of_quarter[...], fine_block(own, lon, lat, diag, row, column))
        block = (tokens_m[cell].astype(F32) + added).astype(BF)
        stream[cell] = block
        hat, _ = norm_parts(members(block.astype(F32)))
        merged[32 * cell : 32 * cell + 32, :] = (hat * gain_merge[...]).astype(BF)
    for step in range(4):
        total[:, 256 * step : 256 * step + 256] = nn(merged[...], weight_columns(w_merge, 64, 2 * step, 2))
    values = total[...].astype(BF)
    coarse[...] = values
    hat, _ = norm_parts(values.astype(F32))
    normed = (hat * gain2[...]).astype(BF)
    for cell, row, column in coarse_quarters():
        put_quarters(own_o, lon_o, lat_o, diag_o, row, column, normed[32 * cell : 32 * cell + 32])


def leave(block_of, raw_of_merge, out):
    for band in range(4):
        pair = jnp.concatenate([block_of(2 * band), block_of(2 * band + 1)], axis=0)
        moved = nn(raw_of_merge[...], pair).astype(BF).reshape(3, 6, 16, 512)
        out[:, band * 6 : band * 6 + 6] = moved[:, :, 0:12, :]


def split_kernel(
    own, lon, lat, diag, coarse, stream, cot_m, w_up, gain_up, raw_of_merge,
    out, own_o, lon_o, lat_o, diag_o, spread, result,
):
    added = [behind(own, lon, lat, diag, row, column)[...] for _, row, column in coarse_quarters()]
    upper = (coarse[...].astype(F32) + jnp.concatenate(added, axis=0).astype(F32)).astype(BF)
    for step in range(8):
        spread[:, 256 * step : 256 * step + 256] = nn(upper, weight_columns(w_up, 32, 2 * step, 2))
    pulls = []
    for member in range(4):
        hat, scale = norm_parts(spread[:, 512 * member : 512 * member + 512])
        at = slice(32 * member, 32 * member + 32)
        skip = stream[:, at, :].reshape(256, 512).astype(F32)
        result[:, at, :] = (skip + hat * gain_up[...]).astype(BF).reshape(8, 32, 512)
        pulled = cot_m[:, at, :].reshape(256, 512).astype(F32) * gain_up[...]
        pulls.append(norm_back(hat, scale, pulled).astype(BF))
    pulls = jnp.concatenate(pulls, axis=1)
    for step in range(4):
        part = nt(pulls, weight_rows(w_up, 32, 16, 256 * step, 256)).astype(BF)
        columns = slice(256 * step, 256 * step + 256)
        for cell, row, column in coarse_quarters():
            value = part[32 * cell : 32 * cell + 32]
            own_o[row, column, :, columns] = value
            if column == 0:
                lon_o[row, :, columns] = value
            if row == 0:
                lat_o[column, :, columns] = value
            if cell == 0:
                diag_o[0, :, columns] = value
    leave(lambda cell: result[cell], raw_of_merge, out)


def merge_back_kernel(
    own, lon, lat, diag, upper_grad, coarse, stream, cot_m, w_merge, gain_merge, gain2, quarter_of_merge,
    stream_grad, own_o, lon_o, lat_o, diag_o, pulled,
):
    came = [behind(own, lon, lat, diag, row, column)[...] for _, row, column in coarse_quarters()]
    came = jnp.concatenate(came, axis=0).astype(F32) * gain2[...]
    hat, scale = norm_parts(coarse[...].astype(F32))
    down = norm_back(hat, scale, came)
    grads = [upper_grad[row, column] for _, row, column in coarse_quarters()]
    down = (jnp.concatenate(grads, axis=0).astype(F32) + down).astype(BF)
    for step in range(8):
        columns = slice(256 * step, 256 * step + 256)
        pulled[:, columns] = nt(down, weight_rows(w_merge, 64, 8, 256 * step, 256)).astype(BF)
    for cell, row, column in coarse_quarters():
        hat, scale = norm_parts(members(stream[cell].astype(F32)))
        grad = norm_back(hat, scale, pulled[32 * cell : 32 * cell + 32, :].astype(F32) * gain_merge[...])
        grad = jnp.concatenate([grad[:, 512 * m : 512 * m + 512] for m in range(4)], axis=0)
        grad = (grad + cot_m[cell].astype(F32)).astype(BF)
        stream_grad[cell] = grad
        quarters = nn(quarter_of_merge[...], grad).astype(BF)
        for q in range(4):
            value = quarters[32 * q : 32 * q + 32]
            put_quarters(own_o, lon_o, lat_o, diag_o, 2 * row + q // 2, 2 * column + q % 2, value)


def exit_kernel(
    own, lon, lat, diag, tokens_m, stream_grad, gain, merge_of_quarter, raw_of_merge, out,
):
    def block_of(cell):
        came = nn(merge_of_quarter[...], fine_block(own, lon, lat, diag, cell // 2, cell % 2))
        hat, scale = norm_parts(tokens_m[cell].astype(F32))
        first = norm_back(hat, scale, came * gain[...])
        return (stream_grad[cell].astype(F32) + first).astype(BF)

    leave(block_of, raw_of_merge, out)


WHOLE = pl.BlockSpec(memory_space=pltpu.VMEM)


def part_of(name):
    first, rows, tiles = PACK[name]
    size = rows * tiles
    return pl.BlockSpec((LONS, size, 128), lambda i: (0, first // size, 0), pipeline_mode=pl.Buffered(1))


def call(body, outs, scratch, operands, packed=None, scalars=(), flops=10**9, name=None):
    specs, arrays = [], []
    for index, operand in enumerate(operands):
        if isinstance(operand, str):
            specs.append(part_of(operand))
            arrays.append(packed)
        elif index in scalars:
            specs.append(pl.BlockSpec(memory_space=pltpu.SMEM))
            arrays.append(operand)
        else:
            specs.append(WHOLE)
            arrays.append(operand)
    return pl.pallas_call(
        body,
        grid=(1,),
        out_shape=[jax.ShapeDtypeStruct(shape, kind) for shape, kind in outs],
        in_specs=specs,
        out_specs=[WHOLE] * len(outs),
        scratch_shapes=[pltpu.VMEM(shape, kind) for shape, kind in scratch],
        compiler_params=pltpu.CompilerParams(vmem_limit_bytes=56 * MIB),
        cost_estimate=pl.CostEstimate(flops=flops, bytes_accessed=4 * MIB, transcendentals=0),
        name=name,
    )(*arrays)


def field_outs(rows, columns, width):
    return [
        ((rows, columns, 32, width), BF),
        ((rows, 32, width), BF),
        ((columns, 32, width), BF),
        ((1, 32, width), BF),
    ]


def move(pieces, step):
    lon, lat, diag = pieces
    lons, lats = lax.axis_size("lon"), lax.axis_size("lat")
    lon = lax.ppermute(lon, "lon", [(i, (i + step) % lons) for i in range(lons)])
    lat = lax.ppermute(lat, "lat", [(i, (i + step) % lats) for i in range(lats)])
    route = []
    for i in range(lons):
        for j in range(lats):
            route.append((i * lats + j, (i + step) % lons * lats + (j + step) % lats))
    diag = lax.ppermute(diag, ("lon", "lat"), route)
    return lon, lat, diag


def usable_tokens(grid):
    rows, columns = grid.shape
    cells = grid.reshape(rows // 3, 3, columns // 3, 3).transpose(0, 2, 1, 3).reshape(rows // 3, columns // 3, 9)
    cells = jnp.pad(jnp.concatenate([cells] * 3, axis=2), ((0, 0), (0, 0), (0, 5)))
    cells = cells.reshape(rows // 6, 2, columns // 6, 2, 32).transpose(0, 2, 1, 3, 4)
    return cells.reshape(rows // 6 * (columns // 6), 1, 128).astype(F32)


def shards(
    tokens, valid, w_qkv1, w_out1, w_merge, w_qkv2, w_out2, w_up, gain1, gain_merge, gain2, gain_up, out_cot,
):
    (share,) = call(
        pack_kernel, [((PACK_ROWS, 128), BF)], [], [w_qkv1, w_out1, w_merge, w_qkv2, w_out2, w_up], name="pack"
    )
    packed = lax.all_gather(share, "lon", axis=0, tiled=False)
    merge_of_raw, quarter_of_merge = permutations()
    raw_of_merge = jnp.asarray(merge_of_raw.T, BF)
    merge_of_quarter = jnp.asarray(quarter_of_merge.T, BF)
    merge_of_raw = jnp.asarray(merge_of_raw, BF)
    quarter_of_merge = jnp.asarray(quarter_of_merge, BF)
    gain1, gain_merge, gain2, gain_up = (g.reshape(1, -1) for g in (gain1, gain_merge, gain2, gain_up))

    lat_at, lon_at = lax.axis_index("lat"), lax.axis_index("lon")
    wide = jnp.concatenate([valid, valid[:6]], axis=0)
    wide = jnp.concatenate([wide, wide[:, :6]], axis=1)
    near = lax.dynamic_slice(wide, (lat_at * 24, lon_at * 12), (30, 18))
    usable1 = usable_tokens(near[3:27, 3:15])
    usable2 = usable_tokens(jnp.max(near[6:30, 6:18].reshape(12, 2, 6, 2), axis=(1, 3)))
    flag = (lat_at == lax.axis_size("lat") - 1).astype(jnp.int32).reshape(1, 1)

    tokens_m, cot_m, *h1 = call(
        enter_kernel,
        [((8, 128, 512), BF), ((8, 128, 512), BF), *field_outs(8, 4, 512)],
        [((3, 24, 16, 512), BF)],
        [tokens, out_cot, gain1, merge_of_raw, quarter_of_merge],
        name="enter",
    )

    def attend(field, names, usable, name):
        rows, columns, _, width = field[0].shape
        windows, tiles = rows * columns // 4, width // 128
        saved = [
            ((3 * tiles, windows, 128, 128), BF),
            ((windows, tiles, 512, 128), BF),
            ((windows, tiles, 128, 128), F32),
            ((tiles, windows, 128, 128), BF),
        ]
        result = call(
            attend_kernel,
            [*field_outs(rows, columns, width), *saved],
            [((windows, 128, width), BF)],
            [field[0], *move(field[1:], -1), *names, usable, flag],
            packed=packed,
            scalars=(7,),
            name=name,
        )
        return (result[0], *move(result[1:4], 1)), result[4:]

    def attend_back(field, names, saved, name):
        rows, columns, _, width = field[0].shape
        windows, tiles = rows * columns // 4, width // 128
        result = call(
            attend_back_kernel,
            field_outs(rows, columns, width),
            [((windows, 128, width), BF), ((3 * tiles, windows, 128, 128), BF)],
            [field[0], *move(field[1:], -1), *names, *saved],
            packed=packed,
            name=name,
        )
        return (result[0], *move(result[1:4], 1))

    a1, saved1 = attend(h1, ("qkv1", "out1"), usable1, "attend_first")
    stream, coarse, *h2 = call(
        merge_kernel,
        [((8, 128, 512), BF), ((256, 1024), BF), *field_outs(4, 2, 1024)],
        [((256, 2048), BF), ((256, 1024), F32)],
        [*a1, tokens_m, "merge", gain_merge, gain2, merge_of_quarter],
        packed=packed,
        name="merge",
    )
    a2, saved2 = attend(h2, ("qkv2", "out2"), usable2, "attend_second")
    output, *upper_grad = call(
        split_kernel,
        [(tokens.shape, BF), *field_outs(4, 2, 1024)],
        [((256, 2048), F32), ((8, 128, 512), BF)],
        [*a2, coarse, stream, cot_m, "up", gain_up, raw_of_merge],
        packed=packed,
        name="split",
    )
    h2_grad = attend_back(upper_grad, ("qkv2", "out2"), saved2, "attend_second_back")
    stream_grad, *a1_grad = call(
        merge_back_kernel,
        [((8, 128, 512), BF), *field_outs(8, 4, 512)],
        [((256, 2048), BF)],
        [*h2_grad, upper_grad[0], coarse, stream, cot_m, "merge", gain_merge, gain2, quarter_of_merge],
        packed=packed,
        name="merge_back",
    )
    h1_grad = attend_back(a1_grad, ("qkv1", "out1"), saved1, "attend_first_back")
    (grad_tokens,) = call(
        exit_kernel,
        [(tokens.shape, BF)],
        [],
        [*h1_grad, tokens_m, stream_grad, gain1, merge_of_quarter, raw_of_merge],
        name="leave",
    )
    return output, grad_tokens


def solution(mesh):
    placed = (P(None, "lat", "lon", None), P(), *[P("lon", None)] * 6, *[P()] * 4, P(None, "lat", "lon", None))
    return jax.shard_map(
        shards,
        mesh=mesh,
        in_specs=placed,
        out_specs=(P(None, "lat", "lon", None), P(None, "lat", "lon", None)),
        check_vma=False,
    )
```

```python
import functools

import jax
import jax.numpy as jnp
import numpy as np
from jax import lax
from jax.experimental import pallas as pl
from jax.experimental.pallas import tpu as pltpu
from jax.sharding import PartitionSpec as P

EPS = 1e-05
BF = jnp.bfloat16
F32 = jnp.float32
LONS = 32
MIB = 1024 * 1024

PACK = {
    "qkv2": (0, 32, 24),
    "out2": (768, 32, 8),
    "merge": (1024, 64, 8),
    "up": (1536, 32, 16),
    "out1": (2048, 16, 4),
    "qkv1": (2112, 16, 12),
}
PACK_ROWS = 2304
SCALE = 32.0**-0.5
LOG2E = 1.4426950408889634
BLOCKED = -1e30


def permutations():
    merge_of_raw = np.zeros((512, 576), np.float32)
    quarter_of_raw = np.zeros((512, 576), np.float32)
    quarter_of_merge = np.zeros((128, 128), np.float32)
    for level in range(3):
        for row in range(6):
            for column in range(6):
                member = (row % 2) * 2 + column % 2
                merge_at = member * 32 + level * 9 + (row // 2) * 3 + column // 2
                quarter = (row // 3) * 2 + column // 3
                quarter_at = quarter * 32 + level * 9 + (row % 3) * 3 + column % 3
                quarter_of_merge[quarter_at, merge_at] = 1
                for band in range(4):
                    raw_at = level * 192 + column * 32 + band * 6 + row
                    merge_of_raw[band * 128 + merge_at, raw_at] = 1
                    quarter_of_raw[band * 128 + quarter_at, raw_at] = 1
    return merge_of_raw, quarter_of_raw, quarter_of_merge


def nn(a, b):
    return lax.dot_general(a, b, (((1,), (0,)), ((), ())), preferred_element_type=F32)


def nt(a, b):
    return lax.dot_general(a, b, (((1,), (1,)), ((), ())), preferred_element_type=F32)


def tn(a, b):
    return lax.dot_general(a, b, (((0,), (0,)), ((), ())), preferred_element_type=F32)


def weight_columns(ref, rows, tile, count):
    parts = []
    for step in range(count):
        start = pl.multiple_of((tile + step) * rows, rows)
        parts.append(ref[:, pl.ds(start, rows), :].reshape(LONS * rows, 128))
    return jnp.concatenate(parts, axis=1) if count > 1 else parts[0]


def weight_rows(ref, rows, tiles, first, count):
    shards = pl.ds(first // rows, count // rows)
    parts = [ref[shards, tile * rows : (tile + 1) * rows, :].reshape(count, 128) for tile in range(tiles)]
    return jnp.concatenate(parts, axis=1)


def norm_parts(values):
    center = values - jnp.mean(values, axis=-1, keepdims=True)
    scale = lax.rsqrt(jnp.mean(center * center, axis=-1, keepdims=True) + EPS)
    return center * scale, scale


def norm_back(hat, scale, pulled):
    down = jnp.mean(pulled, axis=-1, keepdims=True)
    along = jnp.mean(pulled * hat, axis=-1, keepdims=True)
    return scale * (pulled - down - hat * along)


def pack_kernel(qkv1, out1, merge, qkv2, out2, up, packed):
    for name, ref in (("qkv1", qkv1), ("out1", out1), ("merge", merge), ("qkv2", qkv2), ("out2", out2), ("up", up)):
        first, rows, tiles = PACK[name]
        for tile in range(tiles):
            packed[first + tile * rows : first + (tile + 1) * rows, :] = ref[:, tile * 128 : (tile + 1) * 128]


def ahead(own, lon, lat, diag, row, column):
    rows, columns = own.shape[0], own.shape[1]
    if row < rows and column < columns:
        return own.at[row, column]
    if row < rows:
        return lon.at[row]
    if column < columns:
        return lat.at[column]
    return diag.at[0]


def behind(own, lon, lat, diag, row, column):
    if row and column:
        return own.at[row, column]
    if row:
        return lon.at[row]
    if column:
        return lat.at[column]
    return diag.at[0]


def put_quarters(own, lon, lat, diag, row, column, value, lanes=slice(None)):
    own[row, column, :, lanes] = value
    if column == 0 and row:
        lon[row, :, lanes] = value
    if row == 0 and column:
        lat[column, :, lanes] = value
    if row == 0 and column == 0:
        diag[0, :, lanes] = value


def put_next(own, lon, lat, diag, row, column, value, lanes=slice(None)):
    ahead(own, lon, lat, diag, row + 1, column + 1)[:, lanes] = value


def window_spots(rows, columns):
    for row in range(rows):
        for column in range(columns):
            yield row, column, row // 2 * (columns // 2) + column // 2, (row % 2 * 2 + column % 2) * 32


def enter_kernel(
    tokens, cot, quarter_of_raw, merge_of_raw, own, lon, lat, diag, own_c, lon_c, lat_c, diag_c, padded, send
):
    padded[...] = jnp.zeros_like(padded)
    padded[:, :, 0:24, :] = tokens[...]
    for half in range(2):
        rows = padded[:, half * 6 : half * 6 + 6].reshape(576, 512)
        moved = nn(quarter_of_raw[...], rows).astype(BF)
        for quarter in range(16):
            row, column = quarter // 4 * 2 + quarter % 4 // 2, 2 * half + quarter % 2
            put_quarters(own, lon, lat, diag, row, column, moved[quarter * 32 : quarter * 32 + 32])
    send(0)
    padded[:, :, 0:24, :] = cot[...]
    for half in range(2):
        rows = padded[:, half * 6 : half * 6 + 6].reshape(576, 512)
        moved = nn(merge_of_raw[...], rows).astype(BF)
        for band in range(4):
            put_quarters(own_c, lon_c, lat_c, diag_c, band, half, moved[band * 128 : band * 128 + 128])
    send(1)


def head_masks():
    lane = lax.broadcasted_iota(jnp.int32, (1, 128), 1) // 32
    return [lane == head for head in range(4)]


def window_bias(usable_ref, flag_ref, window, windows, per_band):
    me = lax.broadcasted_iota(jnp.int32, (128, 128), 0)
    key = lax.broadcasted_iota(jnp.int32, (128, 128), 1)
    usable = usable_ref[pl.ds(window, 1), 0, :]
    cut = (flag_ref[0, 0] * jnp.where(window >= windows - per_band, 1, 0)).astype(jnp.int32)
    apart = jnp.where((me // 64) == (key // 64), 0, 1) * cut
    allowed = ((usable > 0.0) | (me == key)) & (apart == 0)
    return jnp.where(allowed, 0.0, BLOCKED)


def attend(field, w_qkv, w_out, usable, flag, qkv, raised, inverse, heads_out, per_band, emit):
    windows, _, width = field.shape
    tiles = width // 128
    shard = width // LONS

    def project(step, carry):
        weight = weight_columns(w_qkv, shard, 2 * step, 2)
        mixed = nn(field[...].reshape(windows * 128, width), weight).astype(BF)
        qkv[2 * step] = mixed[:, :128].reshape(windows, 128, 128)
        qkv[2 * step + 1] = mixed[:, 128:].reshape(windows, 128, 128)
        return carry

    lax.fori_loop(0, 3 * tiles // 2, project, 0)
    masks = head_masks()
    zero = jnp.zeros((), BF)
    ones = jnp.ones((128, 128), BF)

    def window_step(window, carry):
        bias = window_bias(usable, flag, window, windows, per_band)
        bias = jnp.concatenate([bias] * 4, axis=0)

        def tile_step(tile, carry):
            query, keys, values = qkv[tile, window], qkv[tiles + tile, window], qkv[2 * tiles + tile, window]
            queries = jnp.concatenate([jnp.where(mask, query, zero) for mask in masks], axis=0)
            power = jnp.exp2(nt(queries, keys) * (SCALE * LOG2E) + bias).astype(BF)
            raised[window, tile] = power
            side = jnp.concatenate([power[128 * head : 128 * head + 128] for head in range(4)], axis=1)
            stacked = jnp.concatenate(
                [
                    jnp.concatenate([jnp.where(mask, values, zero), jnp.where(mask, ones, zero)], axis=1)
                    for mask in masks
                ],
                axis=0,
            )
            both = nn(side, stacked)
            share = 1.0 / both[:, 128:]
            inverse[window, tile] = share
            heads_out[tile, window] = (both[:, :128] * share).astype(BF)
            return carry

        return lax.fori_loop(0, tiles, tile_step, carry)

    lax.fori_loop(0, windows, window_step, 0)
    heads = jnp.concatenate([heads_out[tile].reshape(windows * 128, 128) for tile in range(tiles)], axis=1)
    for step in range(tiles // 2):
        emit(slice(step * 256, step * 256 + 256), nn(heads, weight_columns(w_out, shard, 2 * step, 2)))


def attend_back(field, w_qkv, w_out, qkv, raised, inverse, heads_out, pulled, emit):
    windows, _, width = field.shape
    tiles = width // 128
    shard = width // LONS
    for step in range(tiles // 2):
        part = nt(field[...].reshape(windows * 128, width), weight_rows(w_out, shard, tiles, 256 * step, 256))
        part = part.astype(BF)
        pulled[2 * step] = part[:, :128].reshape(windows, 128, 128)
        pulled[2 * step + 1] = part[:, 128:].reshape(windows, 128, 128)
    masks = head_masks()
    zero = jnp.zeros((), BF)
    ones = jnp.ones((128, 128), BF)

    def stack(values):
        return jnp.concatenate([jnp.where(mask, values, zero) for mask in masks], axis=0)

    def tile_step(index, carry):
        window, tile = index // tiles, index % tiles
        query, keys, values = qkv[tile, window], qkv[tiles + tile, window], qkv[2 * tiles + tile, window]
        power = raised[window, tile]
        scaled = pulled[tile, window].astype(F32) * inverse[window, tile]
        taken = (scaled * heads_out[tile, window].astype(F32)).astype(BF)
        scaled_rows = stack(scaled.astype(BF))
        left = jnp.concatenate([scaled_rows, stack(-taken)], axis=1)
        slope = nt(left, jnp.concatenate([values, ones], axis=1))
        slope = (power.astype(F32) * slope).astype(BF)
        side = jnp.concatenate([slope[128 * head : 128 * head + 128] for head in range(4)], axis=1)
        pulled[2 * tiles + tile, window] = tn(power, scaled_rows).astype(BF)
        pulled[tiles + tile, window] = (tn(slope, stack(query)) * SCALE).astype(BF)
        pulled[tile, window] = (nn(side, stack(keys)) * SCALE).astype(BF)
        return carry

    lax.fori_loop(0, windows * tiles, tile_step, 0)
    pulls = jnp.concatenate([pulled[tile].reshape(windows * 128, 128) for tile in range(3 * tiles)], axis=1)
    for step in range(tiles // 2):
        emit(slice(step * 256, step * 256 + 256), nt(pulls, weight_rows(w_qkv, shard, 3 * tiles, 256 * step, 256)))


def first_kernel(
    own, lon, lat, diag, gain, w_qkv, w_out, usable, flag,
    own_o, lon_o, lat_o, diag_o, field, qkv, raised, inverse, heads_out, normed, send,
):
    for row, column, window, at in window_spots(8, 4):
        field[window, at : at + 32, :] = ahead(own, lon, lat, diag, row + 1, column + 1)[...]
    for window in range(8):
        hat, _ = norm_parts(field[window].astype(F32))
        normed[window] = (hat * gain[...]).astype(BF)

    def emit(lanes, result):
        result = result.astype(BF).astype(F32)
        for row, column, window, at in window_spots(8, 4):
            start = window * 128 + at
            stream = field[window, at : at + 32, lanes].astype(F32) + result[start : start + 32]
            put_quarters(own_o, lon_o, lat_o, diag_o, row, column, stream.astype(BF), lanes)

    attend(normed, w_qkv, w_out, usable, flag, qkv, raised, inverse, heads_out, 2, emit)
    send(0)


def first_back_kernel(
    own, lon, lat, diag, tokens, gain, w_qkv, w_out, qkv, raised, inverse, heads_out,
    own_o, lon_o, lat_o, diag_o, field, pulled, came, send,
):
    for row, column, window, at in window_spots(8, 4):
        field[window, at : at + 32, :] = behind(own, lon, lat, diag, row, column)[...]

    def emit(lanes, result):
        came[:, :, lanes] = result.reshape(8, 128, 256)

    attend_back(field, w_qkv, w_out, qkv, raised, inverse, heads_out, pulled, emit)
    for window in range(8):
        hat, scale = norm_parts(tokens[window].astype(F32))
        grad = norm_back(hat, scale, came[window] * gain[...])
        came[window] = field[window].astype(F32) + grad
    for row, column, window, at in window_spots(8, 4):
        value = came[window, at : at + 32, :].astype(BF)
        put_next(own_o, lon_o, lat_o, diag_o, row, column, value)
    send(0)


def members(block):
    return jnp.concatenate([block[32 * m : 32 * m + 32] for m in range(4)], axis=1)


def middle_kernel(
    own, lon, lat, diag, own_c, lon_c, lat_c, diag_c, w_merge, w_qkv, w_out, w_up,
    gain_merge, gain2, gain_up, usable, flag, merge_of_quarter, quarter_of_merge,
    own_o, lon_o, lat_o, diag_o, own_r, lon_r, lat_r, diag_r,
    stream, cot, wide, coarse, field, upper, spread, qkv, raised, inverse, heads_out, pulled, total, send,
):
    cells = [(cell, cell // 2, cell % 2) for cell in range(8)]
    for cell, row, column in cells:
        parts = [
            ahead(own, lon, lat, diag, 2 * row + q // 2 + 1, 2 * column + q % 2 + 1)[...] for q in range(4)
        ]
        block = nn(merge_of_quarter[...], jnp.concatenate(parts, axis=0))
        stream[cell] = block.astype(BF)
        cot[cell] = ahead(own_c, lon_c, lat_c, diag_c, row + 1, column + 1)[...]
        hat, _ = norm_parts(members(block))
        wide[32 * cell : 32 * cell + 32, :] = (hat * gain_merge[...]).astype(BF)
    for step in range(4):
        total[:, 256 * step : 256 * step + 256] = nn(wide[...], weight_columns(w_merge, 64, 2 * step, 2))
    values = total[...].astype(BF)
    coarse[...] = values
    hat, _ = norm_parts(values.astype(F32))
    field[...] = (hat * gain2[...]).astype(BF).reshape(2, 128, 1024)

    def add_coarse(lanes, result):
        result = result.astype(BF).astype(F32)
        upper[:, lanes] = (coarse[:, lanes].astype(F32) + result).astype(BF)

    attend(field, w_qkv, w_out, usable, flag, qkv, raised, inverse, heads_out, 1, add_coarse)
    for step in range(8):
        spread[:, 256 * step : 256 * step + 256] = nn(upper[...], weight_columns(w_up, 32, 2 * step, 2))
    for member in range(4):
        lanes = slice(512 * member, 512 * member + 512)
        hat, scale = norm_parts(spread[:, lanes])
        at = slice(32 * member, 32 * member + 32)
        skip = stream[:, at, :].reshape(256, 512).astype(F32)
        result = (skip + hat * gain_up[...]).astype(BF)
        for cell, row, column in cells:
            ahead(own_r, lon_r, lat_r, diag_r, row + 1, column + 1)[at, :] = result[32 * cell : 32 * cell + 32]
        pull = cot[:, at, :].reshape(256, 512).astype(F32) * gain_up[...]
        wide[:, lanes] = norm_back(hat, scale, pull).astype(BF)
    send(1)
    for step in range(4):
        lanes = slice(256 * step, 256 * step + 256)
        part = nt(wide[...], weight_rows(w_up, 32, 16, 256 * step, 256)).astype(BF)
        upper[:, lanes] = part
        field[:, :, lanes] = part.reshape(2, 128, 256)

    def keep(lanes, result):
        total[:, lanes] = result.astype(BF).astype(F32) * gain2[:, lanes]

    attend_back(field, w_qkv, w_out, qkv, raised, inverse, heads_out, pulled, keep)
    hat, scale = norm_parts(coarse[...].astype(F32))
    down = (upper[...].astype(F32) + norm_back(hat, scale, total[...])).astype(BF)
    for step in range(8):
        lanes = slice(256 * step, 256 * step + 256)
        wide[:, lanes] = nt(down, weight_rows(w_merge, 64, 8, 256 * step, 256)).astype(BF)
    for cell, row, column in cells:
        hat, scale = norm_parts(members(stream[cell].astype(F32)))
        grad = norm_back(hat, scale, wide[32 * cell : 32 * cell + 32, :].astype(F32) * gain_merge[...])
        grad = jnp.concatenate([grad[:, 512 * m : 512 * m + 512] for m in range(4)], axis=0)
        grad = (grad + cot[cell].astype(F32)).astype(BF)
        quarters = nn(quarter_of_merge[...], grad).astype(BF)
        for q in range(4):
            value = quarters[32 * q : 32 * q + 32]
            put_next(own_o, lon_o, lat_o, diag_o, 2 * row + q // 2, 2 * column + q % 2, value)
    send(0)


def leave_kernel(
    own, lon, lat, diag, own_r, lon_r, lat_r, diag_r, raw_of_quarter, raw_of_merge, grad, out,
):
    for half in range(2):
        parts = []
        for quarter in range(16):
            row, column = quarter // 4 * 2 + quarter % 4 // 2, 2 * half + quarter % 2
            parts.append(behind(own, lon, lat, diag, row, column)[...])
        moved = nn(raw_of_quarter[...], jnp.concatenate(parts, axis=0)).astype(BF).reshape(3, 6, 32, 512)
        grad[:, half * 6 : half * 6 + 6] = moved[:, :, 0:24, :]
        parts = [behind(own_r, lon_r, lat_r, diag_r, band, half)[...] for band in range(4)]
        moved = nn(raw_of_merge[...], jnp.concatenate(parts, axis=0)).astype(BF).reshape(3, 6, 32, 512)
        out[:, half * 6 : half * 6 + 6] = moved[:, :, 0:24, :]


WHOLE = pl.BlockSpec(memory_space=pltpu.VMEM)


def part_of(name):
    first, rows, tiles = PACK[name]
    size = rows * tiles
    return pl.BlockSpec((LONS, size, 128), lambda i: (0, first // size, 0), pipeline_mode=pl.Buffered(1))


def neighbours(step):
    lons, lats = lax.axis_size("lon"), lax.axis_size("lat")
    lon = lax.rem(lax.axis_index("lon") + (lons + step), lons)
    lat = lax.rem(lax.axis_index("lat") + (lats + step), lats)
    here = (lax.axis_index("lon"), lax.axis_index("lat"))
    return (lon, here[1]), (here[0], lat), (lon, lat)


def exchanging(body, ins, outs, moves, step):
    def kernel(*refs):
        operands, results, scratch = refs[:ins], list(refs[ins : ins + outs]), refs[ins + outs :]
        count = 3 * len(moves)
        pieces, send_sems, recv_sems = scratch[-count - 2 : -2], scratch[-2], scratch[-1]
        barrier = pltpu.get_barrier_semaphore()
        for device in neighbours(-step):
            pl.semaphore_signal(barrier, inc=1, device_id=device, device_id_type=pl.DeviceIdType.MESH)
        groups = []
        for group, at in enumerate(moves):
            copies = []
            for index, device in enumerate(neighbours(step)):
                source, target = pieces[3 * group + index], results[at + index]
                results[at + index] = source
                if index < 2:
                    used = pl.ds(1, source.shape[0] - 1)
                    source, target = source.at[used], target.at[used]
                copies.append(
                    pltpu.make_async_remote_copy(
                        src_ref=source,
                        dst_ref=target,
                        send_sem=send_sems.at[3 * group + index],
                        recv_sem=recv_sems.at[3 * group + index],
                        device_id=device,
                        device_id_type=pl.DeviceIdType.MESH,
                    )
                )
            groups.append(copies)
        greeted = []

        def send(group):
            if not greeted:
                pl.semaphore_wait(barrier, 3)
                greeted.append(True)
            for copy in groups[group]:
                copy.start()

        body(*operands, *results, *scratch[: -count - 2], send)
        for copies in groups:
            for copy in copies:
                copy.wait()

    return kernel


def call(body, outs, scratch, operands, packed=None, scalars=(), moves=(), step=0, number=0, name=None):
    specs, arrays = [], []
    for index, operand in enumerate(operands):
        if isinstance(operand, str):
            specs.append(part_of(operand))
            arrays.append(packed)
        elif index in scalars:
            specs.append(pl.BlockSpec(memory_space=pltpu.SMEM))
            arrays.append(operand)
        else:
            specs.append(WHOLE)
            arrays.append(operand)
    out_specs = [WHOLE] * len(outs)
    scratch = [pltpu.VMEM(shape, kind) for shape, kind in scratch]
    params = {}
    if moves:
        for at in moves:
            out_specs[at : at + 3] = [pl.BlockSpec(memory_space=pl.ANY)] * 3
            scratch += [pltpu.VMEM(shape, kind) for shape, kind in outs[at : at + 3]]
        scratch += [pltpu.SemaphoreType.DMA((3 * len(moves),))] * 2
        body = exchanging(body, len(operands), len(outs), moves, step)
        params = dict(collective_id=number, has_side_effects=True)
    return pl.pallas_call(
        body,
        grid=(1,),
        out_shape=[jax.ShapeDtypeStruct(shape, kind) for shape, kind in outs],
        in_specs=specs,
        out_specs=out_specs,
        scratch_shapes=scratch,
        compiler_params=pltpu.CompilerParams(vmem_limit_bytes=56 * MIB, **params),
        cost_estimate=pl.CostEstimate(flops=10**9, bytes_accessed=4 * MIB, transcendentals=0),
        name=name,
    )(*arrays)


def field_outs(rows, columns, tokens):
    return [
        ((rows, columns, tokens, 512), BF),
        ((rows, tokens, 512), BF),
        ((columns, tokens, 512), BF),
        ((1, tokens, 512), BF),
    ]


def kept(windows, tiles):
    return [
        ((3 * tiles, windows, 128, 128), BF),
        ((windows, tiles, 512, 128), BF),
        ((windows, tiles, 128, 128), F32),
        ((tiles, windows, 128, 128), BF),
    ]


def turned(field):
    return field.transpose(0, 2, 1, 3)


def usable_tokens(grid):
    rows, columns = grid.shape
    cells = grid.reshape(rows // 3, 3, columns // 3, 3).transpose(0, 2, 1, 3).reshape(rows // 3, columns // 3, 9)
    cells = jnp.pad(jnp.concatenate([cells] * 3, axis=2), ((0, 0), (0, 0), (0, 5)))
    cells = cells.reshape(rows // 6, 2, columns // 6, 2, 32).transpose(0, 2, 1, 3, 4)
    return cells.reshape(rows // 6 * (columns // 6), 1, 128).astype(F32)


def shards(
    tokens, valid, w_qkv1, w_out1, w_merge, w_qkv2, w_out2, w_up, gain1, gain_merge, gain2, gain_up, out_cot,
):
    (share,) = call(
        pack_kernel, [((PACK_ROWS, 128), BF)], [], [w_qkv1, w_out1, w_merge, w_qkv2, w_out2, w_up], name="pack"
    )
    packed = lax.all_gather(share, "lon", axis=0, tiled=False)
    merge_of_raw, quarter_of_raw, quarter_of_merge = (jnp.asarray(m, BF) for m in permutations())
    raw_of_merge, raw_of_quarter, merge_of_quarter = (
        jnp.asarray(np.ascontiguousarray(m.T), BF) for m in permutations()
    )
    gain1, gain_merge, gain2, gain_up = (g.reshape(1, -1) for g in (gain1, gain_merge, gain2, gain_up))

    lat_at, lon_at = lax.axis_index("lat"), lax.axis_index("lon")
    wide = jnp.concatenate([valid, valid[:6]], axis=0)
    wide = jnp.concatenate([wide, wide[:, :6]], axis=1)
    near = lax.dynamic_slice(wide, (lat_at * 24, lon_at * 12), (30, 18))
    usable1 = usable_tokens(near[3:27, 3:15])
    usable2 = usable_tokens(jnp.max(near[6:30, 6:18].reshape(12, 2, 6, 2), axis=(1, 3)))
    flag = (lat_at == lax.axis_size("lat") - 1).astype(jnp.int32).reshape(1, 1)

    fine, whole = field_outs(8, 4, 32), field_outs(4, 2, 128)
    came = call(
        enter_kernel,
        [*fine, *whole],
        [((3, 12, 32, 512), BF)],
        [turned(tokens), turned(out_cot), quarter_of_raw, merge_of_raw],
        moves=(1, 5),
        step=-1,
        number=0,
        name="enter",
    )
    cot = came[4:]
    result = call(
        first_kernel,
        [*fine, ((8, 128, 512), BF), *kept(8, 4)],
        [((8, 128, 512), BF)],
        [*came[:4], gain1, "qkv1", "out1", usable1, flag],
        packed=packed,
        scalars=(8,),
        moves=(1,),
        step=-1,
        number=1,
        name="first",
    )
    stream, windows, saved = result[:4], result[4], result[5:]
    result = call(
        middle_kernel,
        [*fine, *whole],
        [
            ((8, 128, 512), BF),
            ((8, 128, 512), BF),
            ((256, 2048), BF),
            ((256, 1024), BF),
            ((2, 128, 1024), BF),
            ((256, 1024), BF),
            ((256, 2048), F32),
            *kept(2, 8),
            ((24, 2, 128, 128), BF),
            ((256, 1024), F32),
        ],
        [
            *stream, *cot, "merge", "qkv2", "out2", "up",
            gain_merge, gain2, gain_up, usable2, flag, merge_of_quarter, quarter_of_merge,
        ],
        packed=packed,
        scalars=(16,),
        moves=(1, 5),
        step=1,
        number=2,
        name="middle",
    )
    stream_grad, output = result[:4], result[4:]
    grad = call(
        first_back_kernel,
        fine,
        [((8, 128, 512), BF), ((12, 8, 128, 128), BF), ((8, 128, 512), F32)],
        [*stream_grad, windows, gain1, "qkv1", "out1", *saved],
        packed=packed,
        moves=(1,),
        step=1,
        number=3,
        name="first_back",
    )
    grad_tokens, output = call(
        leave_kernel,
        [((3, 12, 24, 512), BF)] * 2,
        [],
        [*grad, *output, raw_of_quarter, raw_of_merge],
        name="leave",
    )
    return turned(output), turned(grad_tokens)


def solution(mesh):
    placed = (P(None, "lat", "lon", None), P(), *[P("lon", None)] * 6, *[P()] * 4, P(None, "lat", "lon", None))
    return jax.shard_map(
        shards,
        mesh=mesh,
        in_specs=placed,
        out_specs=(P(None, "lat", "lon", None), P(None, "lat", "lon", None)),
        check_vma=False,
    )
```

```python
import functools

import jax
import jax.numpy as jnp
import numpy as np
from jax import lax
from jax.experimental import pallas as pl
from jax.experimental.pallas import tpu as pltpu
from jax.sharding import PartitionSpec as P

EPS = 1e-05
BF = jnp.bfloat16
F32 = jnp.float32
LONS = 32
MIB = 1024 * 1024

PACK = {
    "qkv1": (0, 0, 16, 12),
    "out1": (0, 192, 16, 4),
    "qkv2": (1, 0, 32, 24),
    "out2": (1, 768, 32, 8),
    "merge": (1, 1024, 64, 8),
    "up": (1, 1536, 32, 16),
}
SHARE_ROWS = (256, 2048)
ROUNDS = ("z", "p1", "p2", "q1", "q2", "r1", "r2", "r3")
COPIES = 38
SCALE = 32.0**-0.5
LOG2E = 1.4426950408889634
BLOCKED = -1e30


def permutations():
    merge_of_raw = np.zeros((512, 576), np.float32)
    quarter_of_raw = np.zeros((512, 576), np.float32)
    quarter_of_merge = np.zeros((128, 128), np.float32)
    for level in range(3):
        for row in range(6):
            for column in range(6):
                member = (row % 2) * 2 + column % 2
                merge_at = member * 32 + level * 9 + (row // 2) * 3 + column // 2
                quarter = (row // 3) * 2 + column // 3
                quarter_at = quarter * 32 + level * 9 + (row % 3) * 3 + column % 3
                quarter_of_merge[quarter_at, merge_at] = 1
                for band in range(4):
                    raw_at = level * 192 + column * 32 + band * 6 + row
                    merge_of_raw[band * 128 + merge_at, raw_at] = 1
                    quarter_of_raw[band * 128 + quarter_at, raw_at] = 1
    return merge_of_raw, quarter_of_raw, quarter_of_merge


def nn(a, b):
    return lax.dot_general(a, b, (((1,), (0,)), ((), ())), preferred_element_type=F32)


def nt(a, b):
    return lax.dot_general(a, b, (((1,), (1,)), ((), ())), preferred_element_type=F32)


def tn(a, b):
    return lax.dot_general(a, b, (((0,), (0,)), ((), ())), preferred_element_type=F32)


def weight_columns(ref, rows, tile, count):
    parts = []
    for step in range(count):
        start = pl.multiple_of((tile + step) * rows, rows)
        parts.append(ref[:, pl.ds(start, rows), :].reshape(LONS * rows, 128))
    return jnp.concatenate(parts, axis=1) if count > 1 else parts[0]


def weight_rows(ref, rows, tiles, first, count):
    shards = pl.ds(first // rows, count // rows)
    parts = [ref[shards, tile * rows : (tile + 1) * rows, :].reshape(count, 128) for tile in range(tiles)]
    return jnp.concatenate(parts, axis=1)


def norm_parts(values):
    center = values - jnp.mean(values, axis=-1, keepdims=True)
    scale = lax.rsqrt(jnp.mean(center * center, axis=-1, keepdims=True) + EPS)
    return center * scale, scale


def norm_back(hat, scale, pulled):
    down = jnp.mean(pulled, axis=-1, keepdims=True)
    along = jnp.mean(pulled * hat, axis=-1, keepdims=True)
    return scale * (pulled - down - hat * along)


def pack(shares, **weights):
    for name, ref in weights.items():
        share, first, rows, tiles = PACK[name]
        for tile in range(tiles):
            at = slice(first + tile * rows, first + (tile + 1) * rows)
            shares[share][at, :] = ref[:, tile * 128 : (tile + 1) * 128]


def place():
    lon, lat = lax.axis_index("lon"), lax.axis_index("lat")
    return lat % 2 * 2 + lon // 2 % 2, lat // 2, lon // 4, lon % 2


def device_at(x, y, z, core):
    return z * 4 + x % 2 * 2 + core, y * 2 + x // 2


def gather_peers(rounds):
    x, y, z, core = place()
    peers = [device_at(x, y, (z + step) % 8, core) for step in range(1, 8)] if "z" in rounds else []
    peers += [device_at((x + step) % 4, y, z, core) for step in (1, 3)]
    peers += [device_at(x, (y + step) % 4, z, core) for step in (1, 3)]
    return peers + [device_at(x, y, z, 1 - core)]


def gather_rounds(share, whole, send_sems, recv_sems):
    x, y, z, core = place()
    part = whole.shape[3] // 16
    half = 8 * part
    plus_x, minus_x, plus_y, minus_y = (x + 1) % 4, (x + 3) % 4, (y + 1) % 4, (y + 3) % 4
    low, high = pl.ds(0, 4), pl.ds(4, 4)
    every = pl.ds(0, 8)

    def rows(start, count):
        return pl.ds(pl.multiple_of(start, 16), count)

    def one(x, y):
        return rows((y * 2 + x // 2) * part, part)

    def two(x, y):
        return rows(half + (x // 2 * 4 + y) * part, part)

    def slab(which, zs, x, y):
        return whole.at[zs, x % 2, core, which(x, y)]

    def across(zs, y):
        return whole.at[zs, :, core, rows(y * 2 * part, 2 * part)]

    def along(zs, x):
        return whole.at[zs, x % 2, core, rows(half + x // 2 * 4 * part, 4 * part)]

    to = {
        "+x": device_at(plus_x, y, z, core),
        "-x": device_at(minus_x, y, z, core),
        "+y": device_at(x, plus_y, z, core),
        "-y": device_at(x, minus_y, z, core),
        "twin": device_at(x, y, z, 1 - core),
    }
    far_x, far_y = (x + 2) % 4, (y + 2) % 4
    plan = {
        "p1": [
            (slab(one, every, x, y), "+x"),
            (slab(one, every, x, y), "-x"),
            (slab(two, every, x, y), "+y"),
            (slab(two, every, x, y), "-y"),
        ],
        "p2": [
            (slab(one, low, minus_x, y), "+x"),
            (slab(one, high, plus_x, y), "-x"),
            (slab(two, low, x, minus_y), "+y"),
            (slab(two, high, x, plus_y), "-y"),
        ],
        "q1": [(across(every, y), "+y"), (across(every, y), "-y"), (along(every, x), "+x"), (along(every, x), "-x")],
        "q2": [
            (across(low, minus_y), "+y"),
            (across(high, plus_y), "-y"),
            (along(low, minus_x), "+x"),
            (along(high, plus_x), "-x"),
        ],
        "r1": [(across(every, y), "twin"), (along(every, x), "twin")],
        "r2": [
            (across(every, minus_y), "twin"),
            (across(every, plus_y), "twin"),
            (along(every, minus_x), "twin"),
            (along(every, plus_x), "twin"),
        ],
        "r3": [(across(every, far_y), "twin"), (along(every, far_x), "twin")],
    }
    made, count = {"z": [], "own": []}, 0

    def remote(source, target, device):
        nonlocal count
        count += 1
        return pltpu.make_async_remote_copy(
            src_ref=source,
            dst_ref=target,
            send_sem=send_sems.at[count - 1],
            recv_sem=recv_sems.at[count - 1],
            device_id=device,
            device_id_type=pl.DeviceIdType.MESH,
        )

    for which in (one, two):
        here = whole.at[z, x % 2, core, which(x, y)]
        for step in range(1, 8):
            source = here if share is None else share.at[which(x, y)]
            made["z"].append(remote(source, here, device_at(x, y, (z + step) % 8, core)))
        if share is not None:
            own = pltpu.make_async_copy(share.at[which(x, y)], here, send_sems.at[COPIES + len(made["own"])])
            made["own"].append(own)
    for name, copies in plan.items():
        made[name] = [remote(piece, piece, to[device]) for piece, device in copies]
    return made


def start(copies):
    for copy in copies:
        copy.start()


def arrive(copies):
    for copy in copies:
        copy.wait_recv()


def left(copies):
    for copy in copies:
        copy.wait_send()


def ahead(own, lon, lat, diag, row, column):
    rows, columns = own.shape[0], own.shape[1]
    if row < rows and column < columns:
        return own.at[row, column]
    if row < rows:
        return lon.at[row]
    if column < columns:
        return lat.at[column]
    return diag.at[0]


def behind(own, lon, lat, diag, row, column):
    if row and column:
        return own.at[row, column]
    if row:
        return lon.at[row]
    if column:
        return lat.at[column]
    return diag.at[0]


def put_quarters(own, lon, lat, diag, row, column, value, lanes=slice(None)):
    own[row, column, :, lanes] = value
    if column == 0 and row:
        lon[row, :, lanes] = value
    if row == 0 and column:
        lat[column, :, lanes] = value
    if row == 0 and column == 0:
        diag[0, :, lanes] = value


def put_next(own, lon, lat, diag, row, column, value, lanes=slice(None)):
    ahead(own, lon, lat, diag, row + 1, column + 1)[:, lanes] = value


def window_spots(rows, columns):
    for row in range(rows):
        for column in range(columns):
            yield row, column, row // 2 * (columns // 2) + column // 2, (row % 2 * 2 + column % 2) * 32


def enter_kernel(
    tokens, cot, quarter_of_raw, merge_of_raw, qkv1, out1, merge, qkv2, out2, up,
    own, lon, lat, diag, own_c, lon_c, lat_c, diag_c, whole1, whole2,
    padded, share1, share2, sends1, recvs1, sends2, recvs2, greet, send,
):
    shares = (share1, share2)
    pack(shares, qkv1=qkv1, out1=out1)
    first = gather_rounds(share1, whole1, sends1, recvs1)
    rest = gather_rounds(share2, whole2, sends2, recvs2)
    greet()
    start(first["z"] + first["own"])
    padded[...] = jnp.zeros_like(padded)
    padded[:, :, 0:24, :] = tokens[...]
    for half in range(2):
        rows = padded[:, half * 6 : half * 6 + 6].reshape(576, 512)
        moved = nn(quarter_of_raw[...], rows).astype(BF)
        for quarter in range(16):
            row, column = quarter // 4 * 2 + quarter % 4 // 2, 2 * half + quarter % 2
            put_quarters(own, lon, lat, diag, row, column, moved[quarter * 32 : quarter * 32 + 32])
    send(0)
    arrive(first["z"])
    for copy in first["own"]:
        copy.wait()
    start(first["p1"])
    pack(shares, merge=merge, qkv2=qkv2, out2=out2, up=up)
    start(rest["z"] + rest["own"])
    arrive(first["p1"])
    start(first["p2"])
    padded[:, :, 0:24, :] = cot[...]
    for half in range(2):
        rows = padded[:, half * 6 : half * 6 + 6].reshape(576, 512)
        moved = nn(merge_of_raw[...], rows).astype(BF)
        for band in range(4):
            put_quarters(own_c, lon_c, lat_c, diag_c, band, half, moved[band * 128 : band * 128 + 128])
    arrive(first["p2"])
    start(first["q1"] + first["r1"])
    arrive(rest["z"])
    for copy in rest["own"]:
        copy.wait()
    arrive(first["q1"])
    start(first["q2"] + first["r2"])
    start(rest["p1"])
    send(1)
    arrive(first["q2"])
    start(first["r3"])
    arrive(rest["p1"])
    start(rest["p2"])
    arrive(first["r1"] + first["r2"] + first["r3"])
    arrive(rest["p2"])
    for name in ROUNDS:
        left(first[name])
    left(rest["z"] + rest["p1"] + rest["p2"])


def head_masks():
    lane = lax.broadcasted_iota(jnp.int32, (1, 128), 1) // 32
    return [lane == head for head in range(4)]


def window_bias(usable_ref, flag_ref, window, windows, per_band):
    me = lax.broadcasted_iota(jnp.int32, (128, 128), 0)
    key = lax.broadcasted_iota(jnp.int32, (128, 128), 1)
    usable = usable_ref[pl.ds(window, 1), 0, :]
    cut = (flag_ref[0, 0] * jnp.where(window >= windows - per_band, 1, 0)).astype(jnp.int32)
    apart = jnp.where((me // 64) == (key // 64), 0, 1) * cut
    allowed = ((usable > 0.0) | (me == key)) & (apart == 0)
    return jnp.where(allowed, 0.0, BLOCKED)


def attend(field, w_qkv, w_out, usable, flag, qkv, raised, inverse, heads_out, per_band, emit):
    windows, _, width = field.shape
    tiles = width // 128
    shard = width // LONS

    def project(step, carry):
        weight = weight_columns(w_qkv, shard, 2 * step, 2)
        mixed = nn(field[...].reshape(windows * 128, width), weight).astype(BF)
        qkv[2 * step] = mixed[:, :128].reshape(windows, 128, 128)
        qkv[2 * step + 1] = mixed[:, 128:].reshape(windows, 128, 128)
        return carry

    lax.fori_loop(0, 3 * tiles // 2, project, 0)
    masks = head_masks()
    zero = jnp.zeros((), BF)
    ones = jnp.ones((128, 128), BF)

    def window_step(window, carry):
        bias = window_bias(usable, flag, window, windows, per_band)
        bias = jnp.concatenate([bias] * 4, axis=0)

        def tile_step(tile, carry):
            query, keys, values = qkv[tile, window], qkv[tiles + tile, window], qkv[2 * tiles + tile, window]
            queries = jnp.concatenate([jnp.where(mask, query, zero) for mask in masks], axis=0)
            power = jnp.exp2(nt(queries, keys) * (SCALE * LOG2E) + bias).astype(BF)
            raised[window, tile] = power
            side = jnp.concatenate([power[128 * head : 128 * head + 128] for head in range(4)], axis=1)
            stacked = jnp.concatenate(
                [
                    jnp.concatenate([jnp.where(mask, values, zero), jnp.where(mask, ones, zero)], axis=1)
                    for mask in masks
                ],
                axis=0,
            )
            both = nn(side, stacked)
            share = 1.0 / both[:, 128:]
            inverse[window, tile] = share
            heads_out[tile, window] = (both[:, :128] * share).astype(BF)
            return carry

        return lax.fori_loop(0, tiles, tile_step, carry)

    lax.fori_loop(0, windows, window_step, 0)
    heads = jnp.concatenate([heads_out[tile].reshape(windows * 128, 128) for tile in range(tiles)], axis=1)
    for step in range(tiles // 2):
        emit(slice(step * 256, step * 256 + 256), nn(heads, weight_columns(w_out, shard, 2 * step, 2)))


def attend_back(field, w_qkv, w_out, qkv, raised, inverse, heads_out, pulled, emit):
    windows, _, width = field.shape
    tiles = width // 128
    shard = width // LONS
    for step in range(tiles // 2):
        part = nt(field[...].reshape(windows * 128, width), weight_rows(w_out, shard, tiles, 256 * step, 256))
        part = part.astype(BF)
        pulled[2 * step] = part[:, :128].reshape(windows, 128, 128)
        pulled[2 * step + 1] = part[:, 128:].reshape(windows, 128, 128)
    masks = head_masks()
    zero = jnp.zeros((), BF)
    ones = jnp.ones((128, 128), BF)

    def stack(values):
        return jnp.concatenate([jnp.where(mask, values, zero) for mask in masks], axis=0)

    def tile_step(index, carry):
        window, tile = index // tiles, index % tiles
        query, keys, values = qkv[tile, window], qkv[tiles + tile, window], qkv[2 * tiles + tile, window]
        power = raised[window, tile]
        scaled = pulled[tile, window].astype(F32) * inverse[window, tile]
        taken = (scaled * heads_out[tile, window].astype(F32)).astype(BF)
        scaled_rows = stack(scaled.astype(BF))
        left = jnp.concatenate([scaled_rows, stack(-taken)], axis=1)
        slope = nt(left, jnp.concatenate([values, ones], axis=1))
        slope = (power.astype(F32) * slope).astype(BF)
        side = jnp.concatenate([slope[128 * head : 128 * head + 128] for head in range(4)], axis=1)
        pulled[2 * tiles + tile, window] = tn(power, scaled_rows).astype(BF)
        pulled[tiles + tile, window] = (tn(slope, stack(query)) * SCALE).astype(BF)
        pulled[tile, window] = (nn(side, stack(keys)) * SCALE).astype(BF)
        return carry

    lax.fori_loop(0, windows * tiles, tile_step, 0)
    pulls = jnp.concatenate([pulled[tile].reshape(windows * 128, 128) for tile in range(3 * tiles)], axis=1)
    for step in range(tiles // 2):
        emit(slice(step * 256, step * 256 + 256), nt(pulls, weight_rows(w_qkv, shard, 3 * tiles, 256 * step, 256)))


def first_kernel(
    own, lon, lat, diag, gain, w_qkv, w_out, usable, flag, whole_in,
    own_o, lon_o, lat_o, diag_o, field, qkv, raised, inverse, heads_out, whole, normed, sends, recvs, greet, send,
):
    rest = gather_rounds(None, whole, sends, recvs)
    greet()
    start(rest["q1"] + rest["r1"])
    for row, column, window, at in window_spots(8, 4):
        field[window, at : at + 32, :] = ahead(own, lon, lat, diag, row + 1, column + 1)[...]
    for window in range(8):
        hat, _ = norm_parts(field[window].astype(F32))
        normed[window] = (hat * gain[...]).astype(BF)

    def emit(lanes, result):
        result = result.astype(BF).astype(F32)
        for row, column, window, at in window_spots(8, 4):
            start = window * 128 + at
            stream = field[window, at : at + 32, lanes].astype(F32) + result[start : start + 32]
            put_quarters(own_o, lon_o, lat_o, diag_o, row, column, stream.astype(BF), lanes)

    attend(normed, w_qkv, w_out, usable, flag, qkv, raised, inverse, heads_out, 2, emit)
    send(0)
    arrive(rest["q1"])
    start(rest["q2"] + rest["r2"])
    arrive(rest["q2"])
    start(rest["r3"])
    arrive(rest["r1"] + rest["r2"] + rest["r3"])
    for name in ROUNDS[3:]:
        left(rest[name])


def first_back_kernel(
    own, lon, lat, diag, tokens, gain, w_qkv, w_out, qkv, raised, inverse, heads_out,
    own_o, lon_o, lat_o, diag_o, field, pulled, came, greet, send,
):
    for row, column, window, at in window_spots(8, 4):
        field[window, at : at + 32, :] = behind(own, lon, lat, diag, row, column)[...]

    def emit(lanes, result):
        came[:, :, lanes] = result.reshape(8, 128, 256)

    attend_back(field, w_qkv, w_out, qkv, raised, inverse, heads_out, pulled, emit)
    for window in range(8):
        hat, scale = norm_parts(tokens[window].astype(F32))
        grad = norm_back(hat, scale, came[window] * gain[...])
        came[window] = field[window].astype(F32) + grad
    for row, column, window, at in window_spots(8, 4):
        value = came[window, at : at + 32, :].astype(BF)
        put_next(own_o, lon_o, lat_o, diag_o, row, column, value)
    greet()
    send(0)


def members(block):
    return jnp.concatenate([block[32 * m : 32 * m + 32] for m in range(4)], axis=1)


def middle_kernel(
    own, lon, lat, diag, own_c, lon_c, lat_c, diag_c, w_merge, w_qkv, w_out, w_up,
    gain_merge, gain2, gain_up, usable, flag, merge_of_quarter, quarter_of_merge,
    own_o, lon_o, lat_o, diag_o, own_r, lon_r, lat_r, diag_r,
    stream, cot, wide, coarse, field, upper, spread, qkv, raised, inverse, heads_out, pulled, total, greet, send,
):
    cells = [(cell, cell // 2, cell % 2) for cell in range(8)]
    for cell, row, column in cells:
        parts = [
            ahead(own, lon, lat, diag, 2 * row + q // 2 + 1, 2 * column + q % 2 + 1)[...] for q in range(4)
        ]
        block = nn(merge_of_quarter[...], jnp.concatenate(parts, axis=0))
        stream[cell] = block.astype(BF)
        cot[cell] = ahead(own_c, lon_c, lat_c, diag_c, row + 1, column + 1)[...]
        hat, _ = norm_parts(members(block))
        wide[32 * cell : 32 * cell + 32, :] = (hat * gain_merge[...]).astype(BF)
    for step in range(4):
        total[:, 256 * step : 256 * step + 256] = nn(wide[...], weight_columns(w_merge, 64, 2 * step, 2))
    values = total[...].astype(BF)
    coarse[...] = values
    hat, _ = norm_parts(values.astype(F32))
    field[...] = (hat * gain2[...]).astype(BF).reshape(2, 128, 1024)

    def add_coarse(lanes, result):
        result = result.astype(BF).astype(F32)
        upper[:, lanes] = (coarse[:, lanes].astype(F32) + result).astype(BF)

    attend(field, w_qkv, w_out, usable, flag, qkv, raised, inverse, heads_out, 1, add_coarse)
    for step in range(8):
        spread[:, 256 * step : 256 * step + 256] = nn(upper[...], weight_columns(w_up, 32, 2 * step, 2))
    for member in range(4):
        lanes = slice(512 * member, 512 * member + 512)
        hat, scale = norm_parts(spread[:, lanes])
        at = slice(32 * member, 32 * member + 32)
        skip = stream[:, at, :].reshape(256, 512).astype(F32)
        result = (skip + hat * gain_up[...]).astype(BF)
        for cell, row, column in cells:
            ahead(own_r, lon_r, lat_r, diag_r, row + 1, column + 1)[at, :] = result[32 * cell : 32 * cell + 32]
        pull = cot[:, at, :].reshape(256, 512).astype(F32) * gain_up[...]
        wide[:, lanes] = norm_back(hat, scale, pull).astype(BF)
    greet()
    send(1)
    for step in range(4):
        lanes = slice(256 * step, 256 * step + 256)
        part = nt(wide[...], weight_rows(w_up, 32, 16, 256 * step, 256)).astype(BF)
        upper[:, lanes] = part
        field[:, :, lanes] = part.reshape(2, 128, 256)

    def keep(lanes, result):
        total[:, lanes] = result.astype(BF).astype(F32) * gain2[:, lanes]

    attend_back(field, w_qkv, w_out, qkv, raised, inverse, heads_out, pulled, keep)
    hat, scale = norm_parts(coarse[...].astype(F32))
    down = (upper[...].astype(F32) + norm_back(hat, scale, total[...])).astype(BF)
    for step in range(8):
        lanes = slice(256 * step, 256 * step + 256)
        wide[:, lanes] = nt(down, weight_rows(w_merge, 64, 8, 256 * step, 256)).astype(BF)
    for cell, row, column in cells:
        hat, scale = norm_parts(members(stream[cell].astype(F32)))
        grad = norm_back(hat, scale, wide[32 * cell : 32 * cell + 32, :].astype(F32) * gain_merge[...])
        grad = jnp.concatenate([grad[:, 512 * m : 512 * m + 512] for m in range(4)], axis=0)
        grad = (grad + cot[cell].astype(F32)).astype(BF)
        quarters = nn(quarter_of_merge[...], grad).astype(BF)
        for q in range(4):
            value = quarters[32 * q : 32 * q + 32]
            put_next(own_o, lon_o, lat_o, diag_o, 2 * row + q // 2, 2 * column + q % 2, value)
    send(0)


def leave_kernel(
    own, lon, lat, diag, own_r, lon_r, lat_r, diag_r, raw_of_quarter, raw_of_merge, grad, out,
):
    for half in range(2):
        parts = []
        for quarter in range(16):
            row, column = quarter // 4 * 2 + quarter % 4 // 2, 2 * half + quarter % 2
            parts.append(behind(own, lon, lat, diag, row, column)[...])
        moved = nn(raw_of_quarter[...], jnp.concatenate(parts, axis=0)).astype(BF).reshape(3, 6, 32, 512)
        grad[:, half * 6 : half * 6 + 6] = moved[:, :, 0:24, :]
        parts = [behind(own_r, lon_r, lat_r, diag_r, band, half)[...] for band in range(4)]
        moved = nn(raw_of_merge[...], jnp.concatenate(parts, axis=0)).astype(BF).reshape(3, 6, 32, 512)
        out[:, half * 6 : half * 6 + 6] = moved[:, :, 0:24, :]


WHOLE = pl.BlockSpec(memory_space=pltpu.VMEM)


def part_of(name):
    _, first, rows, tiles = PACK[name]
    size = rows * tiles
    return pl.BlockSpec((LONS, size, 128), lambda i: (0, first // size, 0), pipeline_mode=pl.Buffered(1))


def neighbours(step):
    lons, lats = lax.axis_size("lon"), lax.axis_size("lat")
    lon = lax.rem(lax.axis_index("lon") + (lons + step), lons)
    lat = lax.rem(lax.axis_index("lat") + (lats + step), lats)
    here = (lax.axis_index("lon"), lax.axis_index("lat"))
    return (lon, here[1]), (here[0], lat), (lon, lat)


def exchanging(body, ins, outs, moves, step, rounds):
    def kernel(*refs):
        operands, results, scratch = refs[:ins], list(refs[ins : ins + outs]), refs[ins + outs :]
        count = 3 * len(moves)
        pieces, send_sems, recv_sems = scratch[-count - 2 : -2], scratch[-2], scratch[-1]
        barrier = pltpu.get_barrier_semaphore()
        others = gather_peers(rounds) if rounds else []
        for device in [*neighbours(-step), *others]:
            pl.semaphore_signal(barrier, inc=1, device_id=device, device_id_type=pl.DeviceIdType.MESH)
        groups = []
        for group, at in enumerate(moves):
            copies = []
            for index, device in enumerate(neighbours(step)):
                source, target = pieces[3 * group + index], results[at + index]
                results[at + index] = source
                if index < 2:
                    used = pl.ds(1, source.shape[0] - 1)
                    source, target = source.at[used], target.at[used]
                copies.append(
                    pltpu.make_async_remote_copy(
                        src_ref=source,
                        dst_ref=target,
                        send_sem=send_sems.at[3 * group + index],
                        recv_sem=recv_sems.at[3 * group + index],
                        device_id=device,
                        device_id_type=pl.DeviceIdType.MESH,
                    )
                )
            groups.append(copies)
        def greet():
            pl.semaphore_wait(barrier, 3 + len(others))

        def send(group):
            start(groups[group])

        body(*operands, *results, *scratch[: -count - 2], greet, send)
        for copies in groups:
            for copy in copies:
                copy.wait()

    return kernel


def call(body, outs, scratch, operands, packed=None, scalars=(), moves=(), step=0, number=0, rounds=(), wholes=(), name=None):
    specs, arrays = [], []
    for index, operand in enumerate(operands):
        if isinstance(operand, str):
            specs.append(part_of(operand))
            arrays.append(packed[PACK[operand][0]])
        elif index in scalars:
            specs.append(pl.BlockSpec(memory_space=pltpu.SMEM))
            arrays.append(operand)
        else:
            specs.append(WHOLE)
            arrays.append(operand)
    out_specs = [WHOLE] * len(outs)
    scratch = [pltpu.VMEM(*item) if isinstance(item, tuple) else item for item in scratch]
    params, aliases = {}, {}
    for at in wholes:
        out_specs[at] = pl.BlockSpec(memory_space=pl.ANY)
    if rounds and "z" not in rounds:
        specs[-1] = pl.BlockSpec(memory_space=pl.ANY)
        aliases = {len(specs) - 1: wholes[0]}
    if moves:
        for at in moves:
            out_specs[at : at + 3] = [pl.BlockSpec(memory_space=pl.ANY)] * 3
            scratch += [pltpu.VMEM(shape, kind) for shape, kind in outs[at : at + 3]]
        scratch += [pltpu.SemaphoreType.DMA((3 * len(moves),))] * 2
        body = exchanging(body, len(operands), len(outs), moves, step, rounds)
        params = dict(collective_id=number, has_side_effects=True)
    return pl.pallas_call(
        body,
        grid=(1,),
        out_shape=[jax.ShapeDtypeStruct(shape, kind) for shape, kind in outs],
        in_specs=specs,
        out_specs=out_specs,
        scratch_shapes=scratch,
        input_output_aliases=aliases,
        compiler_params=pltpu.CompilerParams(vmem_limit_bytes=56 * MIB, **params),
        cost_estimate=pl.CostEstimate(flops=10**9, bytes_accessed=4 * MIB, transcendentals=0),
        name=name,
    )(*arrays)


def field_outs(rows, columns, tokens):
    return [
        ((rows, columns, tokens, 512), BF),
        ((rows, tokens, 512), BF),
        ((columns, tokens, 512), BF),
        ((1, tokens, 512), BF),
    ]


def kept(windows, tiles):
    return [
        ((3 * tiles, windows, 128, 128), BF),
        ((windows, tiles, 512, 128), BF),
        ((windows, tiles, 128, 128), F32),
        ((tiles, windows, 128, 128), BF),
    ]


def turned(field):
    return field.transpose(0, 2, 1, 3)


def usable_tokens(grid):
    rows, columns = grid.shape
    cells = grid.reshape(rows // 3, 3, columns // 3, 3).transpose(0, 2, 1, 3).reshape(rows // 3, columns // 3, 9)
    cells = jnp.pad(jnp.concatenate([cells] * 3, axis=2), ((0, 0), (0, 0), (0, 5)))
    cells = cells.reshape(rows // 6, 2, columns // 6, 2, 32).transpose(0, 2, 1, 3, 4)
    return cells.reshape(rows // 6 * (columns // 6), 1, 128).astype(F32)


def shards(
    tokens, valid, w_qkv1, w_out1, w_merge, w_qkv2, w_out2, w_up, gain1, gain_merge, gain2, gain_up, out_cot,
):
    merge_of_raw, quarter_of_raw, quarter_of_merge = (jnp.asarray(m, BF) for m in permutations())
    raw_of_merge, raw_of_quarter, merge_of_quarter = (
        jnp.asarray(np.ascontiguousarray(m.T), BF) for m in permutations()
    )
    gain1, gain_merge, gain2, gain_up = (g.reshape(1, -1) for g in (gain1, gain_merge, gain2, gain_up))

    lat_at, lon_at = lax.axis_index("lat"), lax.axis_index("lon")
    wide = jnp.concatenate([valid, valid[:6]], axis=0)
    wide = jnp.concatenate([wide, wide[:, :6]], axis=1)
    near = lax.dynamic_slice(wide, (lat_at * 24, lon_at * 12), (30, 18))
    usable1 = usable_tokens(near[3:27, 3:15])
    usable2 = usable_tokens(jnp.max(near[6:30, 6:18].reshape(12, 2, 6, 2), axis=(1, 3)))
    flag = (lat_at == lax.axis_size("lat") - 1).astype(jnp.int32).reshape(1, 1)

    fine, whole = field_outs(8, 4, 32), field_outs(4, 2, 128)
    came = call(
        enter_kernel,
        [*fine, *whole, *[((8, 2, 2, rows, 128), BF) for rows in SHARE_ROWS]],
        [
            ((3, 12, 32, 512), BF),
            *[((rows, 128), BF) for rows in SHARE_ROWS],
            *[pltpu.SemaphoreType.DMA((COPIES + 2,)), pltpu.SemaphoreType.DMA((COPIES,))] * 2,
        ],
        [
            turned(tokens), turned(out_cot), quarter_of_raw, merge_of_raw,
            w_qkv1, w_out1, w_merge, w_qkv2, w_out2, w_up,
        ],
        moves=(1, 5),
        step=-1,
        number=0,
        rounds=ROUNDS,
        wholes=(8, 9),
        name="enter",
    )
    cot = came[4:8]
    packed = [came[8].reshape(LONS, -1, 128)]
    result = call(
        first_kernel,
        [*fine, ((8, 128, 512), BF), *kept(8, 4), ((8, 2, 2, SHARE_ROWS[1], 128), BF)],
        [((8, 128, 512), BF), pltpu.SemaphoreType.DMA((COPIES,)), pltpu.SemaphoreType.DMA((COPIES,))],
        [*came[:4], gain1, "qkv1", "out1", usable1, flag, came[9]],
        packed=packed,
        scalars=(8,),
        moves=(1,),
        step=-1,
        number=1,
        rounds=ROUNDS[3:],
        wholes=(9,),
        name="first",
    )
    stream, windows, saved = result[:4], result[4], result[5:9]
    packed.append(result[9].reshape(LONS, -1, 128))
    result = call(
        middle_kernel,
        [*fine, *whole],
        [
            ((8, 128, 512), BF),
            ((8, 128, 512), BF),
            ((256, 2048), BF),
            ((256, 1024), BF),
            ((2, 128, 1024), BF),
            ((256, 1024), BF),
            ((256, 2048), F32),
            *kept(2, 8),
            ((24, 2, 128, 128), BF),
            ((256, 1024), F32),
        ],
        [
            *stream, *cot, "merge", "qkv2", "out2", "up",
            gain_merge, gain2, gain_up, usable2, flag, merge_of_quarter, quarter_of_merge,
        ],
        packed=packed,
        scalars=(16,),
        moves=(1, 5),
        step=1,
        number=2,
        name="middle",
    )
    stream_grad, output = result[:4], result[4:]
    grad = call(
        first_back_kernel,
        fine,
        [((8, 128, 512), BF), ((12, 8, 128, 128), BF), ((8, 128, 512), F32)],
        [*stream_grad, windows, gain1, "qkv1", "out1", *saved],
        packed=packed,
        moves=(1,),
        step=1,
        number=3,
        name="first_back",
    )
    grad_tokens, output = call(
        leave_kernel,
        [((3, 12, 24, 512), BF)] * 2,
        [],
        [*grad, *output, raw_of_quarter, raw_of_merge],
        name="leave",
    )
    return turned(output), turned(grad_tokens)


def solution(mesh):
    placed = (P(None, "lat", "lon", None), P(), *[P("lon", None)] * 6, *[P()] * 4, P(None, "lat", "lon", None))
    return jax.shard_map(
        shards,
        mesh=mesh,
        in_specs=placed,
        out_specs=(P(None, "lat", "lon", None), P(None, "lat", "lon", None)),
        check_vma=False,
    )
```

```python
import functools

import jax
import jax.numpy as jnp
import numpy as np
from jax import lax
from jax.experimental import pallas as pl
from jax.experimental.pallas import tpu as pltpu
from jax.sharding import PartitionSpec as P

EPS = 1e-05
BF = jnp.bfloat16
F32 = jnp.float32
LONS = 32
MIB = 1024 * 1024

PACK = {
    "qkv1": (0, 0, 16, 12),
    "out1": (0, 192, 16, 4),
    "qkv2": (1, 0, 32, 24),
    "out2": (1, 768, 32, 8),
    "merge": (1, 1024, 64, 8),
    "up": (1, 1536, 32, 16),
}
SHARE_ROWS = (256, 2048)
ROUNDS = ("z", "p1", "p2", "q1", "q2", "r1", "r2", "r3")
COPIES = 38
SCALE = 32.0**-0.5
LOG2E = 1.4426950408889634
BLOCKED = -1e30


def permutations():
    merge_of_raw = np.zeros((512, 576), np.float32)
    quarter_of_raw = np.zeros((512, 576), np.float32)
    quarter_of_merge = np.zeros((128, 128), np.float32)
    for level in range(3):
        for row in range(6):
            for column in range(6):
                member = (row % 2) * 2 + column % 2
                merge_at = member * 32 + level * 9 + (row // 2) * 3 + column // 2
                quarter = (row // 3) * 2 + column // 3
                quarter_at = quarter * 32 + level * 9 + (row % 3) * 3 + column % 3
                quarter_of_merge[quarter_at, merge_at] = 1
                for band in range(4):
                    raw_at = level * 192 + column * 32 + band * 6 + row
                    merge_of_raw[band * 128 + merge_at, raw_at] = 1
                    quarter_of_raw[band * 128 + quarter_at, raw_at] = 1
    return merge_of_raw, quarter_of_raw, quarter_of_merge


def nn(a, b):
    return lax.dot_general(a, b, (((1,), (0,)), ((), ())), preferred_element_type=F32)


def nt(a, b):
    return lax.dot_general(a, b, (((1,), (1,)), ((), ())), preferred_element_type=F32)


def tn(a, b):
    return lax.dot_general(a, b, (((0,), (0,)), ((), ())), preferred_element_type=F32)


def weight_columns(ref, rows, tile, count):
    parts = []
    for step in range(count):
        start = pl.multiple_of((tile + step) * rows, rows)
        parts.append(ref[:, pl.ds(start, rows), :].reshape(LONS * rows, 128))
    return jnp.concatenate(parts, axis=1) if count > 1 else parts[0]


def weight_rows(ref, rows, tiles, first, count):
    shards = pl.ds(first // rows, count // rows)
    parts = [ref[shards, tile * rows : (tile + 1) * rows, :].reshape(count, 128) for tile in range(tiles)]
    return jnp.concatenate(parts, axis=1)


def norm_parts(values):
    center = values - jnp.mean(values, axis=-1, keepdims=True)
    scale = lax.rsqrt(jnp.mean(center * center, axis=-1, keepdims=True) + EPS)
    return center * scale, scale


def norm_back(hat, scale, pulled):
    down = jnp.mean(pulled, axis=-1, keepdims=True)
    along = jnp.mean(pulled * hat, axis=-1, keepdims=True)
    return scale * (pulled - down - hat * along)


def pack(shares, **weights):
    for name, ref in weights.items():
        share, first, rows, tiles = PACK[name]
        for tile in range(tiles):
            at = slice(first + tile * rows, first + (tile + 1) * rows)
            shares[share][at, :] = ref[:, tile * 128 : (tile + 1) * 128]


def place():
    lon, lat = lax.axis_index("lon"), lax.axis_index("lat")
    return lat % 2 * 2 + lon // 2 % 2, lat // 2, lon // 4, lon % 2


def device_at(x, y, z, core):
    return z * 4 + x % 2 * 2 + core, y * 2 + x // 2


def gather_peers(rounds):
    x, y, z, core = place()
    peers = [device_at(x, y, (z + step) % 8, core) for step in range(1, 8)] if "z" in rounds else []
    peers += [device_at((x + step) % 4, y, z, core) for step in (1, 3)]
    peers += [device_at(x, (y + step) % 4, z, core) for step in (1, 3)]
    return peers + [device_at(x, y, z, 1 - core)]


def gather_rounds(share, whole, send_sems, recv_sems):
    x, y, z, core = place()
    part = whole.shape[3] // 16
    half = 8 * part
    plus_x, minus_x, plus_y, minus_y = (x + 1) % 4, (x + 3) % 4, (y + 1) % 4, (y + 3) % 4
    low, high = pl.ds(0, 4), pl.ds(4, 4)
    every = pl.ds(0, 8)

    def rows(start, count):
        return pl.ds(pl.multiple_of(start, 16), count)

    def one(x, y):
        return rows((y * 2 + x // 2) * part, part)

    def two(x, y):
        return rows(half + (x // 2 * 4 + y) * part, part)

    def slab(which, zs, x, y):
        return whole.at[zs, x % 2, core, which(x, y)]

    def across(zs, y):
        return whole.at[zs, :, core, rows(y * 2 * part, 2 * part)]

    def along(zs, x):
        return whole.at[zs, x % 2, core, rows(half + x // 2 * 4 * part, 4 * part)]

    to = {
        "+x": device_at(plus_x, y, z, core),
        "-x": device_at(minus_x, y, z, core),
        "+y": device_at(x, plus_y, z, core),
        "-y": device_at(x, minus_y, z, core),
        "twin": device_at(x, y, z, 1 - core),
    }
    far_x, far_y = (x + 2) % 4, (y + 2) % 4
    plan = {
        "p1": [
            (slab(one, every, x, y), "+x"),
            (slab(one, every, x, y), "-x"),
            (slab(two, every, x, y), "+y"),
            (slab(two, every, x, y), "-y"),
        ],
        "p2": [
            (slab(one, low, minus_x, y), "+x"),
            (slab(one, high, plus_x, y), "-x"),
            (slab(two, low, x, minus_y), "+y"),
            (slab(two, high, x, plus_y), "-y"),
        ],
        "q1": [(across(every, y), "+y"), (across(every, y), "-y"), (along(every, x), "+x"), (along(every, x), "-x")],
        "q2": [
            (across(low, minus_y), "+y"),
            (across(high, plus_y), "-y"),
            (along(low, minus_x), "+x"),
            (along(high, plus_x), "-x"),
        ],
        "r1": [(across(every, y), "twin"), (along(every, x), "twin")],
        "r2": [
            (across(every, minus_y), "twin"),
            (across(every, plus_y), "twin"),
            (along(every, minus_x), "twin"),
            (along(every, plus_x), "twin"),
        ],
        "r3": [(across(every, far_y), "twin"), (along(every, far_x), "twin")],
    }
    made, count = {"z": [], "own": []}, 0

    def remote(source, target, device):
        nonlocal count
        count += 1
        return pltpu.make_async_remote_copy(
            src_ref=source,
            dst_ref=target,
            send_sem=send_sems.at[count - 1],
            recv_sem=recv_sems.at[count - 1],
            device_id=device,
            device_id_type=pl.DeviceIdType.MESH,
        )

    for which in (one, two):
        here = whole.at[z, x % 2, core, which(x, y)]
        for step in range(1, 8):
            source = here if share is None else share.at[which(x, y)]
            made["z"].append(remote(source, here, device_at(x, y, (z + step) % 8, core)))
        if share is not None:
            own = pltpu.make_async_copy(share.at[which(x, y)], here, send_sems.at[COPIES + len(made["own"])])
            made["own"].append(own)
    for name, copies in plan.items():
        made[name] = [remote(piece, piece, to[device]) for piece, device in copies]
    return made


def start(copies):
    for copy in copies:
        copy.start()


def arrive(copies):
    for copy in copies:
        copy.wait_recv()


def left(copies):
    for copy in copies:
        copy.wait_send()


def ahead(own, lon, lat, diag, row, column):
    rows, columns = own.shape[0], own.shape[1]
    if row < rows and column < columns:
        return own.at[row, column]
    if row < rows:
        return lon.at[row]
    if column < columns:
        return lat.at[column]
    return diag.at[0]


def behind(own, lon, lat, diag, row, column):
    if row and column:
        return own.at[row, column]
    if row:
        return lon.at[row]
    if column:
        return lat.at[column]
    return diag.at[0]


def put_quarters(own, lon, lat, diag, row, column, value, lanes=slice(None)):
    own[row, column, :, lanes] = value
    if column == 0 and row:
        lon[row, :, lanes] = value
    if row == 0 and column:
        lat[column, :, lanes] = value
    if row == 0 and column == 0:
        diag[0, :, lanes] = value


def put_next(own, lon, lat, diag, row, column, value, lanes=slice(None)):
    ahead(own, lon, lat, diag, row + 1, column + 1)[:, lanes] = value


def window_spots(rows, columns):
    for row in range(rows):
        for column in range(columns):
            yield row, column, row // 2 * (columns // 2) + column // 2, (row % 2 * 2 + column % 2) * 32


def enter_kernel(
    tokens, cot, quarter_of_raw, merge_of_raw, qkv1, out1, merge, qkv2, out2, up,
    own, lon, lat, diag, own_c, lon_c, lat_c, diag_c, whole1, whole2,
    padded, share1, share2, sends1, recvs1, sends2, recvs2, greet, send,
):
    shares = (share1, share2)
    pack(shares, qkv1=qkv1, out1=out1)
    first = gather_rounds(share1, whole1, sends1, recvs1)
    rest = gather_rounds(share2, whole2, sends2, recvs2)
    greet()
    start(first["z"] + first["own"])
    padded[...] = jnp.zeros_like(padded)
    padded[:, :, 0:24, :] = tokens[...]
    for half in range(2):
        rows = padded[:, half * 6 : half * 6 + 6].reshape(576, 512)
        moved = nn(quarter_of_raw[...], rows).astype(BF)
        for quarter in range(16):
            row, column = quarter // 4 * 2 + quarter % 4 // 2, 2 * half + quarter % 2
            put_quarters(own, lon, lat, diag, row, column, moved[quarter * 32 : quarter * 32 + 32])
    send(0)
    arrive(first["z"])
    for copy in first["own"]:
        copy.wait()
    start(first["p1"])
    pack(shares, merge=merge, qkv2=qkv2, out2=out2, up=up)
    start(rest["z"] + rest["own"])
    arrive(first["p1"])
    start(first["p2"])
    padded[:, :, 0:24, :] = cot[...]
    for half in range(2):
        rows = padded[:, half * 6 : half * 6 + 6].reshape(576, 512)
        moved = nn(merge_of_raw[...], rows).astype(BF)
        for band in range(4):
            put_quarters(own_c, lon_c, lat_c, diag_c, band, half, moved[band * 128 : band * 128 + 128])
    arrive(first["p2"])
    start(first["q1"] + first["r1"])
    arrive(rest["z"])
    for copy in rest["own"]:
        copy.wait()
    arrive(first["q1"])
    start(first["q2"] + first["r2"])
    start(rest["p1"])
    send(1)
    arrive(first["q2"])
    start(first["r3"])
    arrive(rest["p1"])
    start(rest["p2"])
    arrive(first["r1"] + first["r2"] + first["r3"])
    arrive(rest["p2"])
    for name in ROUNDS:
        left(first[name])
    left(rest["z"] + rest["p1"] + rest["p2"])


def head_masks():
    lane = lax.broadcasted_iota(jnp.int32, (1, 128), 1) // 32
    return [lane == head for head in range(4)]


def window_bias(usable_ref, flag_ref, window, windows, per_band):
    me = lax.broadcasted_iota(jnp.int32, (128, 128), 0)
    key = lax.broadcasted_iota(jnp.int32, (128, 128), 1)
    usable = usable_ref[pl.ds(window, 1), 0, :]
    cut = (flag_ref[0, 0] * jnp.where(window >= windows - per_band, 1, 0)).astype(jnp.int32)
    apart = jnp.where((me // 64) == (key // 64), 0, 1) * cut
    allowed = ((usable > 0.0) | (me == key)) & (apart == 0)
    return jnp.where(allowed, 0.0, BLOCKED)


def attend(field, w_qkv, w_out, usable, flag, qkv, raised, inverse, heads_out, per_band, emit):
    windows, _, width = field.shape
    tiles = width // 128
    shard = width // LONS

    def project(step, carry):
        weight = weight_columns(w_qkv, shard, 2 * step, 2)
        mixed = nn(field[...].reshape(windows * 128, width), weight).astype(BF)
        qkv[2 * step] = mixed[:, :128].reshape(windows, 128, 128)
        qkv[2 * step + 1] = mixed[:, 128:].reshape(windows, 128, 128)
        return carry

    lax.fori_loop(0, 3 * tiles // 2, project, 0)
    masks = head_masks()
    zero = jnp.zeros((), BF)
    ones = jnp.ones((128, 128), BF)

    def window_step(window, carry):
        bias = window_bias(usable, flag, window, windows, per_band)
        bias = jnp.concatenate([bias] * 4, axis=0)

        def weigh(query, keys, values):
            queries = jnp.concatenate([jnp.where(mask, query, zero) for mask in masks], axis=0)
            power = jnp.exp2(nt(queries, keys) * (SCALE * LOG2E) + bias).astype(BF)
            side = jnp.concatenate([power[128 * head : 128 * head + 128] for head in range(4)], axis=1)
            stacked = jnp.concatenate(
                [
                    jnp.concatenate([jnp.where(mask, values, zero), jnp.where(mask, ones, zero)], axis=1)
                    for mask in masks
                ],
                axis=0,
            )
            both = nn(side, stacked)
            share = 1.0 / both[:, 128:]
            return power, share, (both[:, :128] * share).astype(BF)

        def tile_step(step, carry):
            pair = (2 * step, 2 * step + 1)
            loaded = [[qkv[part * tiles + tile, window] for part in range(3)] for tile in pair]
            made = [weigh(*operands) for operands in loaded]
            for tile, (power, share, out) in zip(pair, made):
                raised[window, tile] = power
                inverse[window, tile] = share
                heads_out[tile, window] = out
            return carry

        return lax.fori_loop(0, tiles // 2, tile_step, carry)

    lax.fori_loop(0, windows, window_step, 0)
    heads = jnp.concatenate([heads_out[tile].reshape(windows * 128, 128) for tile in range(tiles)], axis=1)
    for step in range(tiles // 2):
        emit(slice(step * 256, step * 256 + 256), nn(heads, weight_columns(w_out, shard, 2 * step, 2)))


def attend_back(field, w_qkv, w_out, qkv, raised, inverse, heads_out, pulled, emit):
    windows, _, width = field.shape
    tiles = width // 128
    shard = width // LONS
    for step in range(tiles // 2):
        part = nt(field[...].reshape(windows * 128, width), weight_rows(w_out, shard, tiles, 256 * step, 256))
        part = part.astype(BF)
        pulled[2 * step] = part[:, :128].reshape(windows, 128, 128)
        pulled[2 * step + 1] = part[:, 128:].reshape(windows, 128, 128)
    masks = head_masks()
    zero = jnp.zeros((), BF)
    ones = jnp.ones((128, 128), BF)

    def stack(values):
        return jnp.concatenate([jnp.where(mask, values, zero) for mask in masks], axis=0)

    def pull_back(query, keys, values, power, share, out, down):
        scaled = down.astype(F32) * share
        taken = (scaled * out.astype(F32)).astype(BF)
        scaled_rows = stack(scaled.astype(BF))
        left_side = jnp.concatenate([scaled_rows, stack(-taken)], axis=1)
        slope = nt(left_side, jnp.concatenate([values, ones], axis=1))
        slope = (power.astype(F32) * slope).astype(BF)
        side = jnp.concatenate([slope[128 * head : 128 * head + 128] for head in range(4)], axis=1)
        return (
            (nn(side, stack(keys)) * SCALE).astype(BF),
            (tn(slope, stack(query)) * SCALE).astype(BF),
            tn(power, scaled_rows).astype(BF),
        )

    def tile_step(step, carry):
        pair = [((2 * step + side) // tiles, (2 * step + side) % tiles) for side in range(2)]
        loaded = [
            [qkv[part * tiles + tile, window] for part in range(3)]
            + [raised[window, tile], inverse[window, tile], heads_out[tile, window], pulled[tile, window]]
            for window, tile in pair
        ]
        made = [pull_back(*operands) for operands in loaded]
        for (window, tile), grads in zip(pair, made):
            for part in range(3):
                pulled[part * tiles + tile, window] = grads[part]
        return carry

    lax.fori_loop(0, windows * tiles // 2, tile_step, 0)
    pulls = jnp.concatenate([pulled[tile].reshape(windows * 128, 128) for tile in range(3 * tiles)], axis=1)
    for step in range(tiles // 2):
        emit(slice(step * 256, step * 256 + 256), nt(pulls, weight_rows(w_qkv, shard, 3 * tiles, 256 * step, 256)))


def first_kernel(
    own, lon, lat, diag, gain, w_qkv, w_out, usable, flag, whole_in,
    own_o, lon_o, lat_o, diag_o, field, qkv, raised, inverse, heads_out, whole, normed, sends, recvs, greet, send,
):
    rest = gather_rounds(None, whole, sends, recvs)
    greet()
    start(rest["q1"] + rest["r1"])
    for row, column, window, at in window_spots(8, 4):
        field[window, at : at + 32, :] = ahead(own, lon, lat, diag, row + 1, column + 1)[...]
    for window in range(8):
        hat, _ = norm_parts(field[window].astype(F32))
        normed[window] = (hat * gain[...]).astype(BF)

    def emit(lanes, result):
        result = result.astype(BF).astype(F32)
        for row, column, window, at in window_spots(8, 4):
            start = window * 128 + at
            stream = field[window, at : at + 32, lanes].astype(F32) + result[start : start + 32]
            put_quarters(own_o, lon_o, lat_o, diag_o, row, column, stream.astype(BF), lanes)

    attend(normed, w_qkv, w_out, usable, flag, qkv, raised, inverse, heads_out, 2, emit)
    send(0)
    arrive(rest["q1"])
    start(rest["q2"] + rest["r2"])
    arrive(rest["q2"])
    start(rest["r3"])
    arrive(rest["r1"] + rest["r2"] + rest["r3"])
    for name in ROUNDS[3:]:
        left(rest[name])


def first_back_kernel(
    own, lon, lat, diag, tokens, gain, w_qkv, w_out, qkv, raised, inverse, heads_out,
    own_o, lon_o, lat_o, diag_o, field, pulled, came, greet, send,
):
    for row, column, window, at in window_spots(8, 4):
        field[window, at : at + 32, :] = behind(own, lon, lat, diag, row, column)[...]

    def emit(lanes, result):
        came[:, :, lanes] = result.reshape(8, 128, 256)

    attend_back(field, w_qkv, w_out, qkv, raised, inverse, heads_out, pulled, emit)
    for window in range(8):
        hat, scale = norm_parts(tokens[window].astype(F32))
        grad = norm_back(hat, scale, came[window] * gain[...])
        came[window] = field[window].astype(F32) + grad
    for row, column, window, at in window_spots(8, 4):
        value = came[window, at : at + 32, :].astype(BF)
        put_next(own_o, lon_o, lat_o, diag_o, row, column, value)
    greet()
    send(0)


def members(block):
    return jnp.concatenate([block[32 * m : 32 * m + 32] for m in range(4)], axis=1)


def middle_kernel(
    own, lon, lat, diag, own_c, lon_c, lat_c, diag_c, w_merge, w_qkv, w_out, w_up,
    gain_merge, gain2, gain_up, usable, flag, merge_of_quarter, quarter_of_merge,
    own_o, lon_o, lat_o, diag_o, own_r, lon_r, lat_r, diag_r,
    stream, cot, wide, coarse, field, upper, spread, qkv, raised, inverse, heads_out, pulled, total, greet, send,
):
    cells = [(cell, cell // 2, cell % 2) for cell in range(8)]
    for cell, row, column in cells:
        parts = [
            ahead(own, lon, lat, diag, 2 * row + q // 2 + 1, 2 * column + q % 2 + 1)[...] for q in range(4)
        ]
        block = nn(merge_of_quarter[...], jnp.concatenate(parts, axis=0))
        stream[cell] = block.astype(BF)
        cot[cell] = ahead(own_c, lon_c, lat_c, diag_c, row + 1, column + 1)[...]
        hat, _ = norm_parts(members(block))
        wide[32 * cell : 32 * cell + 32, :] = (hat * gain_merge[...]).astype(BF)
    for step in range(4):
        total[:, 256 * step : 256 * step + 256] = nn(wide[...], weight_columns(w_merge, 64, 2 * step, 2))
    values = total[...].astype(BF)
    coarse[...] = values
    hat, _ = norm_parts(values.astype(F32))
    field[...] = (hat * gain2[...]).astype(BF).reshape(2, 128, 1024)

    def add_coarse(lanes, result):
        result = result.astype(BF).astype(F32)
        upper[:, lanes] = (coarse[:, lanes].astype(F32) + result).astype(BF)

    attend(field, w_qkv, w_out, usable, flag, qkv, raised, inverse, heads_out, 1, add_coarse)
    for step in range(8):
        spread[:, 256 * step : 256 * step + 256] = nn(upper[...], weight_columns(w_up, 32, 2 * step, 2))
    for member in range(4):
        lanes = slice(512 * member, 512 * member + 512)
        hat, scale = norm_parts(spread[:, lanes])
        at = slice(32 * member, 32 * member + 32)
        skip = stream[:, at, :].reshape(256, 512).astype(F32)
        result = (skip + hat * gain_up[...]).astype(BF)
        for cell, row, column in cells:
            ahead(own_r, lon_r, lat_r, diag_r, row + 1, column + 1)[at, :] = result[32 * cell : 32 * cell + 32]
        pull = cot[:, at, :].reshape(256, 512).astype(F32) * gain_up[...]
        wide[:, lanes] = norm_back(hat, scale, pull).astype(BF)
    greet()
    send(1)
    for step in range(4):
        lanes = slice(256 * step, 256 * step + 256)
        part = nt(wide[...], weight_rows(w_up, 32, 16, 256 * step, 256)).astype(BF)
        upper[:, lanes] = part
        field[:, :, lanes] = part.reshape(2, 128, 256)

    def keep(lanes, result):
        total[:, lanes] = result.astype(BF).astype(F32) * gain2[:, lanes]

    attend_back(field, w_qkv, w_out, qkv, raised, inverse, heads_out, pulled, keep)
    hat, scale = norm_parts(coarse[...].astype(F32))
    down = (upper[...].astype(F32) + norm_back(hat, scale, total[...])).astype(BF)
    for step in range(8):
        lanes = slice(256 * step, 256 * step + 256)
        wide[:, lanes] = nt(down, weight_rows(w_merge, 64, 8, 256 * step, 256)).astype(BF)
    for cell, row, column in cells:
        hat, scale = norm_parts(members(stream[cell].astype(F32)))
        grad = norm_back(hat, scale, wide[32 * cell : 32 * cell + 32, :].astype(F32) * gain_merge[...])
        grad = jnp.concatenate([grad[:, 512 * m : 512 * m + 512] for m in range(4)], axis=0)
        grad = (grad + cot[cell].astype(F32)).astype(BF)
        quarters = nn(quarter_of_merge[...], grad).astype(BF)
        for q in range(4):
            value = quarters[32 * q : 32 * q + 32]
            put_next(own_o, lon_o, lat_o, diag_o, 2 * row + q // 2, 2 * column + q % 2, value)
    send(0)


def leave_kernel(
    own, lon, lat, diag, own_r, lon_r, lat_r, diag_r, raw_of_quarter, raw_of_merge, grad, out,
):
    for half in range(2):
        parts = []
        for quarter in range(16):
            row, column = quarter // 4 * 2 + quarter % 4 // 2, 2 * half + quarter % 2
            parts.append(behind(own, lon, lat, diag, row, column)[...])
        moved = nn(raw_of_quarter[...], jnp.concatenate(parts, axis=0)).astype(BF).reshape(3, 6, 32, 512)
        grad[:, half * 6 : half * 6 + 6] = moved[:, :, 0:24, :]
        parts = [behind(own_r, lon_r, lat_r, diag_r, band, half)[...] for band in range(4)]
        moved = nn(raw_of_merge[...], jnp.concatenate(parts, axis=0)).astype(BF).reshape(3, 6, 32, 512)
        out[:, half * 6 : half * 6 + 6] = moved[:, :, 0:24, :]


WHOLE = pl.BlockSpec(memory_space=pltpu.VMEM)


def part_of(name):
    _, first, rows, tiles = PACK[name]
    size = rows * tiles
    return pl.BlockSpec((LONS, size, 128), lambda i: (0, first // size, 0), pipeline_mode=pl.Buffered(1))


def neighbours(step):
    lons, lats = lax.axis_size("lon"), lax.axis_size("lat")
    lon = lax.rem(lax.axis_index("lon") + (lons + step), lons)
    lat = lax.rem(lax.axis_index("lat") + (lats + step), lats)
    here = (lax.axis_index("lon"), lax.axis_index("lat"))
    return (lon, here[1]), (here[0], lat), (lon, lat)


def exchanging(body, ins, outs, moves, step, rounds):
    def kernel(*refs):
        operands, results, scratch = refs[:ins], list(refs[ins : ins + outs]), refs[ins + outs :]
        count = 3 * len(moves)
        pieces, send_sems, recv_sems = scratch[-count - 2 : -2], scratch[-2], scratch[-1]
        barrier = pltpu.get_barrier_semaphore()
        others = gather_peers(rounds) if rounds else []
        for device in [*neighbours(-step), *others]:
            pl.semaphore_signal(barrier, inc=1, device_id=device, device_id_type=pl.DeviceIdType.MESH)
        groups = []
        for group, at in enumerate(moves):
            copies = []
            for index, device in enumerate(neighbours(step)):
                source, target = pieces[3 * group + index], results[at + index]
                results[at + index] = source
                if index < 2:
                    used = pl.ds(1, source.shape[0] - 1)
                    source, target = source.at[used], target.at[used]
                copies.append(
                    pltpu.make_async_remote_copy(
                        src_ref=source,
                        dst_ref=target,
                        send_sem=send_sems.at[3 * group + index],
                        recv_sem=recv_sems.at[3 * group + index],
                        device_id=device,
                        device_id_type=pl.DeviceIdType.MESH,
                    )
                )
            groups.append(copies)
        def greet():
            pl.semaphore_wait(barrier, 3 + len(others))

        def send(group):
            start(groups[group])

        body(*operands, *results, *scratch[: -count - 2], greet, send)
        for copies in groups:
            for copy in copies:
                copy.wait()

    return kernel


def call(body, outs, scratch, operands, packed=None, scalars=(), moves=(), step=0, number=0, rounds=(), wholes=(), name=None):
    specs, arrays = [], []
    for index, operand in enumerate(operands):
        if isinstance(operand, str):
            specs.append(part_of(operand))
            arrays.append(packed[PACK[operand][0]])
        elif index in scalars:
            specs.append(pl.BlockSpec(memory_space=pltpu.SMEM))
            arrays.append(operand)
        else:
            specs.append(WHOLE)
            arrays.append(operand)
    out_specs = [WHOLE] * len(outs)
    scratch = [pltpu.VMEM(*item) if isinstance(item, tuple) else item for item in scratch]
    params, aliases = {}, {}
    for at in wholes:
        out_specs[at] = pl.BlockSpec(memory_space=pl.ANY)
    if rounds and "z" not in rounds:
        specs[-1] = pl.BlockSpec(memory_space=pl.ANY)
        aliases = {len(specs) - 1: wholes[0]}
    if moves:
        for at in moves:
            out_specs[at : at + 3] = [pl.BlockSpec(memory_space=pl.ANY)] * 3
            scratch += [pltpu.VMEM(shape, kind) for shape, kind in outs[at : at + 3]]
        scratch += [pltpu.SemaphoreType.DMA((3 * len(moves),))] * 2
        body = exchanging(body, len(operands), len(outs), moves, step, rounds)
        params = dict(collective_id=number, has_side_effects=True)
    return pl.pallas_call(
        body,
        grid=(1,),
        out_shape=[jax.ShapeDtypeStruct(shape, kind) for shape, kind in outs],
        in_specs=specs,
        out_specs=out_specs,
        scratch_shapes=scratch,
        input_output_aliases=aliases,
        compiler_params=pltpu.CompilerParams(vmem_limit_bytes=56 * MIB, **params),
        cost_estimate=pl.CostEstimate(flops=10**9, bytes_accessed=4 * MIB, transcendentals=0),
        name=name,
    )(*arrays)


def field_outs(rows, columns, tokens):
    return [
        ((rows, columns, tokens, 512), BF),
        ((rows, tokens, 512), BF),
        ((columns, tokens, 512), BF),
        ((1, tokens, 512), BF),
    ]


def kept(windows, tiles):
    return [
        ((3 * tiles, windows, 128, 128), BF),
        ((windows, tiles, 512, 128), BF),
        ((windows, tiles, 128, 128), F32),
        ((tiles, windows, 128, 128), BF),
    ]


def turned(field):
    return field.transpose(0, 2, 1, 3)


def usable_tokens(grid):
    rows, columns = grid.shape
    cells = grid.reshape(rows // 3, 3, columns // 3, 3).transpose(0, 2, 1, 3).reshape(rows // 3, columns // 3, 9)
    cells = jnp.pad(jnp.concatenate([cells] * 3, axis=2), ((0, 0), (0, 0), (0, 5)))
    cells = cells.reshape(rows // 6, 2, columns // 6, 2, 32).transpose(0, 2, 1, 3, 4)
    return cells.reshape(rows // 6 * (columns // 6), 1, 128).astype(F32)


def shards(
    tokens, valid, w_qkv1, w_out1, w_merge, w_qkv2, w_out2, w_up, gain1, gain_merge, gain2, gain_up, out_cot,
):
    merge_of_raw, quarter_of_raw, quarter_of_merge = (jnp.asarray(m, BF) for m in permutations())
    raw_of_merge, raw_of_quarter, merge_of_quarter = (
        jnp.asarray(np.ascontiguousarray(m.T), BF) for m in permutations()
    )
    gain1, gain_merge, gain2, gain_up = (g.reshape(1, -1) for g in (gain1, gain_merge, gain2, gain_up))

    lat_at, lon_at = lax.axis_index("lat"), lax.axis_index("lon")
    wide = jnp.concatenate([valid, valid[:6]], axis=0)
    wide = jnp.concatenate([wide, wide[:, :6]], axis=1)
    near = lax.dynamic_slice(wide, (lat_at * 24, lon_at * 12), (30, 18))
    usable1 = usable_tokens(near[3:27, 3:15])
    usable2 = usable_tokens(jnp.max(near[6:30, 6:18].reshape(12, 2, 6, 2), axis=(1, 3)))
    flag = (lat_at == lax.axis_size("lat") - 1).astype(jnp.int32).reshape(1, 1)

    fine, whole = field_outs(8, 4, 32), field_outs(4, 2, 128)
    came = call(
        enter_kernel,
        [*fine, *whole, *[((8, 2, 2, rows, 128), BF) for rows in SHARE_ROWS]],
        [
            ((3, 12, 32, 512), BF),
            *[((rows, 128), BF) for rows in SHARE_ROWS],
            *[pltpu.SemaphoreType.DMA((COPIES + 2,)), pltpu.SemaphoreType.DMA((COPIES,))] * 2,
        ],
        [
            turned(tokens), turned(out_cot), quarter_of_raw, merge_of_raw,
            w_qkv1, w_out1, w_merge, w_qkv2, w_out2, w_up,
        ],
        moves=(1, 5),
        step=-1,
        number=0,
        rounds=ROUNDS,
        wholes=(8, 9),
        name="enter",
    )
    cot = came[4:8]
    packed = [came[8].reshape(LONS, -1, 128)]
    result = call(
        first_kernel,
        [*fine, ((8, 128, 512), BF), *kept(8, 4), ((8, 2, 2, SHARE_ROWS[1], 128), BF)],
        [((8, 128, 512), BF), pltpu.SemaphoreType.DMA((COPIES,)), pltpu.SemaphoreType.DMA((COPIES,))],
        [*came[:4], gain1, "qkv1", "out1", usable1, flag, came[9]],
        packed=packed,
        scalars=(8,),
        moves=(1,),
        step=-1,
        number=1,
        rounds=ROUNDS[3:],
        wholes=(9,),
        name="first",
    )
    stream, windows, saved = result[:4], result[4], result[5:9]
    packed.append(result[9].reshape(LONS, -1, 128))
    result = call(
        middle_kernel,
        [*fine, *whole],
        [
            ((8, 128, 512), BF),
            ((8, 128, 512), BF),
            ((256, 2048), BF),
            ((256, 1024), BF),
            ((2, 128, 1024), BF),
            ((256, 1024), BF),
            ((256, 2048), F32),
            *kept(2, 8),
            ((24, 2, 128, 128), BF),
            ((256, 1024), F32),
        ],
        [
            *stream, *cot, "merge", "qkv2", "out2", "up",
            gain_merge, gain2, gain_up, usable2, flag, merge_of_quarter, quarter_of_merge,
        ],
        packed=packed,
        scalars=(16,),
        moves=(1, 5),
        step=1,
        number=2,
        name="middle",
    )
    stream_grad, output = result[:4], result[4:]
    grad = call(
        first_back_kernel,
        fine,
        [((8, 128, 512), BF), ((12, 8, 128, 128), BF), ((8, 128, 512), F32)],
        [*stream_grad, windows, gain1, "qkv1", "out1", *saved],
        packed=packed,
        moves=(1,),
        step=1,
        number=3,
        name="first_back",
    )
    grad_tokens, output = call(
        leave_kernel,
        [((3, 12, 24, 512), BF)] * 2,
        [],
        [*grad, *output, raw_of_quarter, raw_of_merge],
        name="leave",
    )
    return turned(output), turned(grad_tokens)


def solution(mesh):
    placed = (P(None, "lat", "lon", None), P(), *[P("lon", None)] * 6, *[P()] * 4, P(None, "lat", "lon", None))
    return jax.shard_map(
        shards,
        mesh=mesh,
        in_specs=placed,
        out_specs=(P(None, "lat", "lon", None), P(None, "lat", "lon", None)),
        check_vma=False,
    )
```
